32 devices in a mesh: row: 2 (over y), blk: 16 (over z, x, core).
Axes of the slice: x: 2, y: 2, z: 4, core: 2. Of those that a mesh axis runs over, the one named last changes fastest.
Arguments:
- coarse_cluster_means: bfloat16 [32768, 1024], P('blk', 'row'), may hold values from -16 to 16
- fine_cluster_means: bfloat16 [4096, 1024], P(('blk', 'row')), may hold values from -6 to 6
- block_panel_candidates: int32 [256, 8], P(('blk', 'row')), may hold values from 0 to 15, all different within a row; in each aligned block of 8 rows (0 to 7, 8 to 15, ...) at most 8 rows name the same one
- softmax_heat: float32 [1], replicated, may hold values from 0.5 to 1
Outputs:
- revised_centroids: bfloat16 [4096, 1024], P(('blk', 'row'))
- log_norm: float32 [32768], P(('blk', 'row'))
The draws below stay inside these ranges and needn't reach their ends.
Inputs may be any that keep to these rules, and one draw needn't show every extreme that they name: `block_panel_candidates`: each row names 8 different panels; within the rows of one device no panel is named by more than 8 rows, and in some device one panel is named by exactly 8 rows.
All inputs are finite; a program needn't handle non-finite values.
Results may differ from the reference program's by a relative error of at most 0.013.
Values may be sent and summed in bfloat16 or wider, within the bound.
A program may use at most 128 MiB of HBM per device.

```python
import math
import jax
import jax.numpy as jnp
import numpy as np
from jax import lax

FEATURE_DIMENSION = 1024
PANEL = 128
BLOCK = 128
PAIRS = 8
BLK_DEV = 8
MOST = 8
POINTS = 32768
ROW_BLOCKS = 256
CENTROIDS = 4096
N_ROW = 2
N_BLK = 16


def draw_coarse_cluster_means(key, part):
    noise = jax.random.normal(jax.random.fold_in(key, 1), (POINTS, FEATURE_DIMENSION), jnp.float32)
    values = jnp.clip(noise, -6.0, 6.0)
    return values.astype(jnp.bfloat16)


def draw_fine_cluster_means(key, part):
    noise = jax.random.normal(jax.random.fold_in(key, 2), (CENTROIDS, FEATURE_DIMENSION), jnp.float32)
    values = jnp.clip(noise, -6.0, 6.0)
    return values.astype(jnp.bfloat16)


def shared_out(rng, own, number, rows, amount, top, most, slope):
    order = jax.random.permutation(rng, amount)
    heavy_load, common = portions_of(amount, rows * top, most, slope, True), portions_of(amount, rows * top, most, slope, False)
    places = jnp.arange(amount)

    def named(lengths, rotation):
        used = int((lengths > 0).sum())
        fixed = max(1, used // 4)
        shifted = fixed + (places - fixed + rotation * (used - fixed)) % max(1, amount - fixed)
        return jnp.zeros((amount,), jnp.int32).at[order[jnp.where(places < fixed, places, shifted)]].set(jnp.asarray(lengths, jnp.int32))

    lengths = jnp.where(number % 4 == 0, named(heavy_load, number // 4), named(common, number - number // 4 - 1))
    mixed = jax.random.permutation(jax.random.fold_in(own, 3), amount)
    donor, taker = mixed[0:amount // 2 * 2:2], mixed[1:amount // 2 * 2:2]
    margin = jnp.minimum(lengths[donor] - 1, most - lengths[taker]) // 2
    margin = jnp.where((donor == order[0]) | (taker == order[0]) | (lengths[taker] == 0), 0, jnp.maximum(margin, 0))
    shifted = jax.random.randint(jax.random.fold_in(own, 4), (amount // 2,), 0, 1 << 20) % (margin + 1)
    lengths = lengths.at[donor].add(-shifted).at[taker].add(shifted)
    labels = jnp.searchsorted(jnp.cumsum(lengths), jnp.arange(rows * top), side="right").astype(jnp.int32)
    grid = labels.reshape(top, rows).T
    grid = grid[jax.random.permutation(jax.random.fold_in(own, 1), rows)]
    rotation = jax.random.randint(jax.random.fold_in(own, 2), (rows, 1), 0, top)
    return jnp.take_along_axis(grid, (jnp.arange(top)[None, :] + rotation) % top, axis=1)


def portions_of(count, total, reach, skew, full):
    loads = [(1 << 20) // math.isqrt(standing ** skew) + 1 for standing in range(1, count + 1)]
    largest = reach if full else min(reach, max(-(-total // count), total * loads[0] // sum(loads)))
    least = 1 if total - largest >= count - 1 else 0
    counts, rest = [largest] + [least] * (count - 1), total - largest - least * (count - 1)
    while rest > 0:
        candidates = [i for i in range(1, count) if counts[i] < largest] or [i for i in range(1, count) if counts[i] < reach]
        pool, budget = sum([loads[i] for i in candidates]), rest
        for i in candidates:
            addition = min(reach - counts[i], max(1, budget * loads[i] // pool), rest)
            counts[i] = counts[i] + addition
            rest = rest - addition
    return np.array(counts)


def setup_inputs(seed: int = 0) -> dict:
    arg_keys = jax.random.split(jax.random.key(seed), 5)
    coarse_cluster_means = draw_coarse_cluster_means(jax.random.fold_in(arg_keys[4], 71), 0)
    fine_cluster_means = draw_fine_cluster_means(jax.random.fold_in(arg_keys[4], 71), 0)
    block_panel_candidates_keys = jax.random.split(jax.random.fold_in(arg_keys[2], 1), ROW_BLOCKS // BLK_DEV)
    block_panel_candidates_turns = jax.random.permutation(jax.random.fold_in(arg_keys[2], 3), ROW_BLOCKS // BLK_DEV)
    block_panel_candidates = jax.vmap(lambda own, number: shared_out(jax.random.fold_in(arg_keys[2], 2), own, number, BLK_DEV, N_BLK, PAIRS, MOST, 2))(block_panel_candidates_keys, block_panel_candidates_turns).reshape((ROW_BLOCKS, PAIRS))
    softmax_heat = jnp.clip(jnp.exp(jax.random.uniform(arg_keys[3], (1,), jnp.float32, math.log(0.5), math.log(1.0))), 0.5, 1.0)
    return dict(coarse_cluster_means=coarse_cluster_means, fine_cluster_means=fine_cluster_means, block_panel_candidates=block_panel_candidates, softmax_heat=softmax_heat)


def reference(coarse_cluster_means, fine_cluster_means, block_panel_candidates, softmax_heat):
    normalizing_multiplier = 1.0 / (softmax_heat[0] * math.sqrt(FEATURE_DIMENSION))
    panel_count = CENTROIDS // PANEL
    blocks = coarse_cluster_means.reshape(ROW_BLOCKS, BLOCK, FEATURE_DIMENSION)
    panels = fine_cluster_means.reshape(panel_count, PANEL, FEATURE_DIMENSION)
    sqnorm = lax.optimization_barrier(jnp.sum(jnp.square(fine_cluster_means.astype(jnp.float32)), axis=1)).reshape(panel_count, PANEL)

    def one_block(index):
        coarse = index // BLK_DEV % N_ROW
        chosen = (jnp.take(block_panel_candidates, index, axis=0) * N_ROW + coarse).astype(jnp.int32)
        cands = jnp.take(panels, chosen, axis=0).reshape(PAIRS * PANEL, FEATURE_DIMENSION)
        norms = jnp.take(sqnorm, chosen, axis=0).reshape(PAIRS * PANEL)
        rows = jnp.take(blocks, index, axis=0)
        dots = jnp.dot(rows.astype(jnp.float32), cands.astype(jnp.float32).T, precision=lax.Precision.HIGHEST)
        logit = (2.0 * dots - norms[None, :]) * normalizing_multiplier
        top = lax.optimization_barrier(jnp.max(logit, axis=1, keepdims=True))
        lse = top[:, 0] + jnp.log(lax.optimization_barrier(jnp.sum(jnp.exp(logit - top), axis=1)))
        assign_weight = jnp.exp(logit - lse[:, None]).astype(jnp.bfloat16)
        sums = jnp.dot(assign_weight.astype(jnp.float32).T, rows.astype(jnp.float32), precision=lax.Precision.HIGHEST)
        mass = lax.optimization_barrier(jnp.sum(assign_weight.astype(jnp.float32), axis=0))
        return (lse, chosen, sums.reshape(PAIRS, PANEL, FEATURE_DIMENSION), mass.reshape(PAIRS, PANEL))

    def step_fn(carry, index):
        acc_sums, acc_mass = carry
        lse, chosen, sums, mass = one_block(index)
        return ((acc_sums.at[chosen].add(sums), acc_mass.at[chosen].add(mass)), lse)
    init = (jnp.zeros((panel_count, PANEL, FEATURE_DIMENSION), jnp.float32), jnp.zeros((panel_count, PANEL), jnp.float32))
    (acc_sums, acc_mass), lses = lax.scan(step_fn, init, jnp.arange(ROW_BLOCKS, dtype=jnp.int32))
    sums = acc_sums.reshape(CENTROIDS, FEATURE_DIMENSION)
    mass = acc_mass.reshape(CENTROIDS)
    updated = ((sums + fine_cluster_means.astype(jnp.float32)) / (mass[:, None] + 1.0)).astype(jnp.bfloat16)
    return (updated, lses.reshape(POINTS))
```

```python
import math

import jax
import jax.numpy as jnp
from jax import lax
from jax.sharding import PartitionSpec as P


def shards(coarse, fine, candidates, heat):
    points = lax.all_to_all(coarse, "row", split_axis=0, concat_axis=1, tiled=True)
    panels = lax.all_gather(fine, "blk", axis=0, tiled=True)
    rows, width = points.shape
    blocks = candidates.shape[0]
    count = lax.axis_size("blk")
    scale = 1.0 / (heat[0] * math.sqrt(width))
    sqnorm = jnp.sum(jnp.square(panels.astype(jnp.float32)), axis=1)
    dots = jnp.einsum("pd,rd->pr", panels, points, preferred_element_type=jnp.float32)
    logit = (2.0 * dots - sqnorm[:, None]) * scale
    named = jnp.any(candidates[None, :, :] == jnp.arange(count)[:, None, None], axis=2)
    logit = logit.reshape(count, -1, blocks, rows // blocks)
    logit = jnp.where(named[:, None, :, None], logit, -jnp.inf).reshape(-1, rows)
    top = jnp.max(logit, axis=0)
    log_norm = top + jnp.log(jnp.sum(jnp.exp(logit - top), axis=0))
    weight = jnp.exp(logit - log_norm).astype(jnp.bfloat16)
    sums = jnp.dot(weight, points, preferred_element_type=jnp.float32)
    mass = jnp.sum(weight.astype(jnp.float32), axis=1)
    sums = lax.psum_scatter(sums, "blk", scatter_dimension=0, tiled=True)
    mass = lax.psum_scatter(mass, "blk", scatter_dimension=0, tiled=True)
    new = (sums + fine.astype(jnp.float32)) / (mass[:, None] + 1.0)
    return new.astype(jnp.bfloat16), log_norm


def solution(mesh):
    return jax.shard_map(
        shards,
        mesh=mesh,
        in_specs=(P("blk", "row"), P(("blk", "row"), None), P(("blk", "row"), None), P()),
        out_specs=(P(("blk", "row"), None), P(("blk", "row"))),
        check_vma=False,
    )
```

```python
import functools
import math

import jax
import jax.numpy as jnp
from jax import lax
from jax.experimental import pallas as pl
from jax.experimental.pallas import tpu as pltpu
from jax.sharding import PartitionSpec as P

MESH = pl.DeviceIdType.MESH
F32 = jnp.float32
BF16 = jnp.bfloat16
LANES = 256


def kernel(
    dims, n_row, x_ref, fine_ref, bias_ref, heat_ref, out_ref, lse_ref,
    xbuf, panels, logits, norms, top, total, weights, part, in_c, send_b, in_b, send_a, in_a,
    mass_out, mass_in,
    x_send, x_recv, g_send, g_recv, c_send, c_recv, b_send, b_recv, a_send, a_recv, m_send, m_recv,
    own_sem,
):
    d0, d1, d2 = dims
    n_blk = d0 * d1 * d2
    row = lax.axis_index("row")
    blk = lax.axis_index("blk")
    i2 = lax.rem(blk, d2)
    i1 = lax.rem(lax.div(blk, d2), d1)
    i0 = lax.div(blk, d1 * d2)
    size = fine_ref.shape[0]
    width = fine_ref.shape[1]
    rows = xbuf.shape[1]
    feats = xbuf.shape[2]
    pair = d2 * size
    chunks = x_send.shape[1]
    step = rows // chunks

    def at(o0, o1, o2, sign):
        a = lax.rem(i0 + sign * o0 + d0, d0)
        b = lax.rem(i1 + sign * o1 + d1, d1)
        c = lax.rem(i2 + sign * o2 + d2, d2)
        return (a * d1 + b) * d2 + c

    def panel(owner, ref):
        return ref.at[pl.ds(pl.multiple_of(owner * size, size), size), :]

    def base_of(o0, o1, sign):
        a = lax.rem(i0 + sign * o0 + d0, d0)
        b = lax.rem(i1 + sign * o1 + d1, d1)
        return (a * d1 + b) * d2

    def remote(src, dst, send, recv, to):
        copy = pltpu.make_async_remote_copy(
            src_ref=src, dst_ref=dst, send_sem=send, recv_sem=recv,
            device_id=to, device_id_type=MESH,
        )
        copy.start()
        return copy

    barrier = pltpu.get_barrier_semaphore()
    for d in range(1, n_row):
        pl.semaphore_signal(
            barrier, inc=1, device_id={"row": lax.rem(row + d, n_row)}, device_id_type=MESH
        )
    for d in range(1, n_blk):
        pl.semaphore_signal(
            barrier, inc=1, device_id={"blk": lax.rem(blk + d, n_blk)}, device_id_type=MESH
        )
    own_x = pltpu.make_async_copy(
        x_ref.at[pl.ds(pl.multiple_of(row * rows, rows), rows), :], xbuf.at[row], own_sem.at[0]
    )
    own_x.start()
    own_panel = pltpu.make_async_copy(fine_ref, panel(blk, panels), own_sem.at[1])
    own_panel.start()
    pl.semaphore_wait(barrier, n_row - 1 + n_blk - 1)

    gathered = {}

    def gather(o, axis, hop):
        final = list(o)
        final[axis] = hop
        final = tuple(final)
        move = [0, 0, 0]
        move[axis] = hop
        owner = at(*o, -1)
        src = fine_ref if o == (0, 0, 0) else panel(owner, panels)
        gathered[final] = remote(
            src, panel(owner, panels), g_send.at[final], g_recv.at[final],
            {"blk": at(*move, 1)},
        )

    for o1 in range(1, d1):
        gather((0, 0, 0), 1, o1)
    for o0 in range(1, d0):
        gather((0, 0, 0), 0, o0)
    for o2 in range(1, d2):
        gather((0, 0, 0), 2, o2)
    points = []
    for c in range(chunks):
        for d in range(1, n_row):
            to = lax.rem(row + d, n_row)
            points.append(remote(
                x_ref.at[pl.ds(pl.multiple_of(to * rows + c * step, step), step), :],
                xbuf.at[row, pl.ds(c * step, step), :],
                x_send.at[d - 1, c], x_recv.at[d - 1, c], {"row": to},
            ))

    def score(o0, o1):
        for o2 in range(1, d2):
            gathered[(o0, o1, o2)].wait_recv()
        base = pl.multiple_of(base_of(o0, o1, -1) * size, pair)
        whole = panels[pl.ds(base, pair), :].astype(F32)
        norms[pl.ds(base, pair), :] = jnp.broadcast_to(
            jnp.sum(whole * whole, axis=1, keepdims=True), (pair, 128)
        )
        left = panels[pl.ds(base, pair), pl.ds(pl.multiple_of(row * feats, feats), feats)]

        @pl.loop(0, rows // LANES)
        def _(c):
            lane = pl.multiple_of(c * LANES, LANES)
            logits[pl.ds(base, pair), pl.ds(lane, LANES)] = lax.dot_general(
                left, xbuf[row, pl.ds(lane, LANES), :], (((1,), (1,)), ((), ())),
                preferred_element_type=F32,
            )

    own_x.wait()
    own_panel.wait()
    order = [(0, 0)] + [(0, o1) for o1 in range(1, d1)] + [(o0, 0) for o0 in range(1, d0)]
    order += [(o0, o1) for o0 in range(1, d0) for o1 in range(1, d1)]
    before = None
    for o0, o1 in order:
        if (o0, o1) != (0, 0):
            gathered[(o0, o1, 0)].wait_recv()
            if o1 == 0:
                for hop in range(1, d1):
                    gather((o0, 0, 0), 1, hop)
            for hop in range(1, d2):
                gather((o0, o1, 0), 2, hop)
        if before is not None:
            score(*before)
        before = (o0, o1)
    score(*before)
    for copy in points:
        copy.wait_recv()

    top[...] = jnp.full(top.shape, -1e30, F32)
    total[...] = jnp.zeros(total.shape, F32)
    scale = 1.0 / (jnp.full((1, LANES), heat_ref[0], F32) * math.sqrt(width))
    tiles = rows // LANES

    @pl.loop(0, n_blk // d2 * tiles)
    def _(t):
        g = lax.div(t, tiles)
        lane = pl.multiple_of(lax.rem(t, tiles) * LANES, LANES)
        base = pl.multiple_of(g * pair, pair)
        dots = logits[pl.ds(base, pair), pl.ds(lane, LANES)]
        for d in range(1, n_row):
            other = lax.rem(row + d, n_row)
            dots += lax.dot_general(
                panels[pl.ds(base, pair), pl.ds(pl.multiple_of(other * feats, feats), feats)],
                xbuf[other, pl.ds(lane, LANES), :], (((1,), (1,)), ((), ())),
                preferred_element_type=F32,
            )
        for j in range(d2):
            value = (2.0 * dots[j * size:(j + 1) * size] - norms[pl.ds(base + j * size, size), :1]) * scale
            value = value + bias_ref[g * d2 + j, :, pl.ds(lane, LANES)]
            logits[pl.ds(base + j * size, size), pl.ds(lane, LANES)] = value
            best = jnp.max(value.reshape(size // 8, 8, LANES), axis=0)
            top[:, pl.ds(lane, LANES)] = jnp.maximum(top[:, pl.ds(lane, LANES)], best)

    peak = jnp.max(top[...], axis=0, keepdims=True)
    top[...] = jnp.broadcast_to(peak, top.shape)

    @pl.loop(0, n_blk)
    def _(g):
        base = pl.multiple_of(g * size, size)
        value = jnp.exp(logits[pl.ds(base, size), :] - top[0:1, :])
        logits[pl.ds(base, size), :] = value
        total[...] += jnp.sum(value.reshape(size // 8, 8, rows), axis=0)

    summed = jnp.sum(total[...], axis=0, keepdims=True)
    lse_ref[...] = top[0:1, :] + jnp.log(summed)
    total[...] = jnp.broadcast_to(1.0 / summed, total.shape)

    masses = []
    sent_c = {}
    sent_b = {}
    sent_a = {}

    def weigh(o0, o1):
        owner = base_of(o0, o1, 1)
        base = pl.multiple_of(owner * size, pair)
        k = o0 * d1 + o1

        weights[...] = (logits[pl.ds(base, pair), :] * total[0:1, :]).astype(BF16)

        @pl.loop(0, n_row)
        def _(s):
            part[k, :, pl.ds(pl.multiple_of(s * feats, feats), feats)] = jnp.dot(
                weights[...], xbuf[s], preferred_element_type=F32
            ).astype(BF16)

        for o2 in range(1, d2):
            j = lax.rem(i2 + o2, d2)
            sent_c[(o0, o1, o2)] = remote(
                part.at[k, pl.ds(pl.multiple_of(j * size, size), size), :],
                in_c.at[k, o2 - 1], c_send.at[k, o2 - 1], c_recv.at[k, o2 - 1],
                {"blk": at(0, 0, o2, 1)},
            )
        mass = lax.dot_general(
            jnp.ones((8, rows), BF16), weights[...], (((1,), (1,)), ((), ())),
            preferred_element_type=F32,
        )
        for j in range(d2):
            mass_out[owner + j] = mass[:, j * size:(j + 1) * size]
        for o2 in range(d2):
            if (o0, o1, o2) != (0, 0, 0):
                to = at(o0, o1, o2, 1)
                masses.append(remote(
                    mass_out.at[to], mass_in.at[blk],
                    m_send.at[o0, o1, o2], m_recv.at[o0, o1, o2], {"blk": to},
                ))

    def chip_sum(o0, o1):
        k = o0 * d1 + o1
        value = part[k, pl.ds(pl.multiple_of(i2 * size, size), size), :].astype(F32)
        for o2 in range(1, d2):
            sent_c[(o0, o1, o2)].wait_recv()
            value = value + in_c[k, o2 - 1].astype(F32)
        if o1 > 0:
            send_b[o0, o1 - 1] = value.astype(BF16)
            sent_b[(o0, o1)] = remote(
                send_b.at[o0, o1 - 1], in_b.at[o0, o1 - 1],
                b_send.at[o0, o1 - 1], b_recv.at[o0, o1 - 1], {"blk": at(0, o1, 0, 1)},
            )
            return None
        for hop in range(1, d1):
            sent_b[(o0, hop)].wait_recv()
            value = value + in_b[o0, hop - 1].astype(F32)
        if o0 > 0:
            send_a[o0 - 1] = value.astype(BF16)
            sent_a[o0] = remote(
                send_a.at[o0 - 1], in_a.at[o0 - 1],
                a_send.at[o0 - 1], a_recv.at[o0 - 1], {"blk": at(o0, 0, 0, 1)},
            )
            return None
        return value

    outer = list(range(1, d0)) + [0]
    order = [(o0, o1) for o1 in range(1, d1) for o0 in outer] + [(o0, 0) for o0 in outer]
    before = None
    for o0, o1 in order:
        weigh(o0, o1)
        if before is not None:
            chip_sum(*before)
        before = (o0, o1)
    value = chip_sum(*before)

    mass_in[blk] = mass_out[blk]
    for copy in masses:
        copy.wait_recv()
    mass = mass_in[0]
    for g in range(1, n_blk):
        mass = mass + mass_in[g]
    column = jnp.broadcast_to(mass[0:1, :], (size, size)).T[:, 0:1]
    value = value + panels[pl.ds(pl.multiple_of(blk * size, size), size), :].astype(F32)
    for o0 in range(1, d0):
        sent_a[o0].wait_recv()
        value = value + in_a[o0 - 1].astype(F32)
    out_ref[...] = (value / (column + 1.0)).astype(BF16)
    for group in (gathered, sent_c, sent_b, sent_a):
        for copy in group.values():
            copy.wait_send()
    for copy in points + masses:
        copy.wait_send()


def shards(n_blk, n_row, coarse, fine, candidates, heat):
    inner = 2 if n_blk < 32 else 4
    dims = (n_blk // (inner * inner), inner, inner)
    d0, d1, d2 = dims
    blocks = candidates.shape[0]
    size, width = fine.shape
    rows = coarse.shape[0] // n_row
    feats = coarse.shape[1]
    ids = jnp.arange(n_blk, dtype=jnp.int32)
    named = jnp.any(candidates[None, :, :] == ids[:, None, None], axis=2)
    bias = jnp.where(named, 0.0, -1e30).astype(F32)
    bias = jnp.repeat(bias, rows // blocks, axis=1).reshape(n_blk, 1, rows)
    vmem = pl.BlockSpec(memory_space=pltpu.VMEM)
    hbm = pl.BlockSpec(memory_space=pl.ANY)
    groups = d0 * d1
    chunks = 4
    dma = pltpu.SemaphoreType.DMA
    new, log_norm = pl.pallas_call(
        functools.partial(kernel, dims, n_row),
        out_shape=(
            jax.ShapeDtypeStruct((size, width), BF16),
            jax.ShapeDtypeStruct((1, rows), F32),
        ),
        in_specs=[hbm, hbm, vmem, pl.BlockSpec(memory_space=pltpu.SMEM)],
        out_specs=(vmem, vmem),
        scratch_shapes=[
            pltpu.VMEM((n_row, rows, feats), BF16),
            pltpu.VMEM((n_blk * size, width), BF16),
            pltpu.VMEM((n_blk * size, rows), F32),
            pltpu.VMEM((n_blk * size, 128), F32),
            pltpu.VMEM((8, rows), F32),
            pltpu.VMEM((8, rows), F32),
            pltpu.VMEM((d2 * size, rows), BF16),
            pltpu.VMEM((groups, d2 * size, width), BF16),
            pltpu.VMEM((groups, d2 - 1, size, width), BF16),
            pltpu.VMEM((d0, d1 - 1, size, width), BF16),
            pltpu.VMEM((d0, d1 - 1, size, width), BF16),
            pltpu.VMEM((d0 - 1, size, width), BF16),
            pltpu.VMEM((d0 - 1, size, width), BF16),
            pltpu.VMEM((n_blk, 8, size), F32),
            pltpu.VMEM((n_blk, 8, size), F32),
            dma((n_row - 1, chunks)), dma((n_row - 1, chunks)),
            dma(dims), dma(dims),
            dma((groups, d2 - 1)), dma((groups, d2 - 1)),
            dma((d0, d1 - 1)), dma((d0, d1 - 1)),
            dma((d0 - 1,)), dma((d0 - 1,)),
            dma(dims), dma(dims),
            dma((2,)),
        ],
        compiler_params=pltpu.CompilerParams(
            collective_id=0, has_side_effects=True, vmem_limit_bytes=60 << 20
        ),
        cost_estimate=pl.CostEstimate(
            flops=4 * rows * n_blk * size * width, bytes_accessed=8 << 20,
            transcendentals=rows * n_blk * size,
        ),
    )(coarse, fine, bias, heat)
    return new, log_norm.reshape(rows)


def solution(mesh):
    return jax.shard_map(
        functools.partial(shards, mesh.shape["blk"], mesh.shape["row"]),
        mesh=mesh,
        in_specs=(P("blk", "row"), P(("blk", "row"), None), P(("blk", "row"), None), P()),
        out_specs=(P(("blk", "row"), None), P(("blk", "row"))),
        check_vma=False,
    )
```

```python
import functools
import math

import jax
import jax.numpy as jnp
from jax import lax
from jax.experimental import pallas as pl
from jax.experimental.pallas import tpu as pltpu
from jax.sharding import PartitionSpec as P

MESH = pl.DeviceIdType.MESH
F32 = jnp.float32
BF16 = jnp.bfloat16
LANES = 256
DEPTH = 3


def kernel(
    dims, n_row, x_ref, fine_ref, named_ref, heat_ref, out_ref, lse_ref,
    xbuf, panels, logits, norms, bias, top, peaks, total, weights, part, in_c, send_b, in_b,
    send_a, in_a, acc, mass_out, mass_in,
    x_send, x_recv, z_send, z_recv, gx_send, gx_recv, gc_send, gc_recv, c_send, c_recv,
    b_send, b_recv, a_send, a_recv, m_send, m_recv, own_sem,
):
    d0, d1, d2 = dims
    n_blk = d0 * d1 * d2
    row = lax.axis_index("row")
    blk = lax.axis_index("blk")
    i2 = lax.rem(blk, d2)
    i1 = lax.rem(lax.div(blk, d2), d1)
    i0 = lax.div(blk, d1 * d2)
    size = fine_ref.shape[0]
    width = fine_ref.shape[1]
    rows = xbuf.shape[1]
    feats = xbuf.shape[2]
    pair = d2 * size
    half = size // 2
    chunks = x_send.shape[1]
    step = rows // chunks
    blocks, names = named_ref.shape

    def near(i, o, d):
        return lax.rem(i + o + d, d)

    def index(a, b, c):
        return (a * d1 + b) * d2 + c

    def panel(owner):
        return panels.at[pl.ds(pl.multiple_of(owner * size, size), size), :]

    def remote(src, dst, send, recv, to, axis="blk"):
        return pltpu.make_async_remote_copy(
            src_ref=src, dst_ref=dst, send_sem=send, recv_sem=recv,
            device_id={axis: to}, device_id_type=MESH,
        )

    barrier = pltpu.get_barrier_semaphore()
    for d in range(1, n_row):
        pl.semaphore_signal(
            barrier, inc=1, device_id={"row": near(row, d, n_row)}, device_id_type=MESH
        )
    for d in range(1, n_blk):
        pl.semaphore_signal(
            barrier, inc=1, device_id={"blk": near(blk, d, n_blk)}, device_id_type=MESH
        )
    own_x = pltpu.make_async_copy(
        x_ref.at[pl.ds(pl.multiple_of(row * rows, rows), rows), :], xbuf.at[row], own_sem.at[0]
    )
    own_x.start()
    own_panel = pltpu.make_async_copy(fine_ref, panel(blk), own_sem.at[1])
    own_panel.start()
    pl.semaphore_wait(barrier, n_row - 1 + n_blk - 1)

    def z_copy(way, k, own=False):
        sign = 1 - 2 * way
        owner = index(i0 - sign * (k - 1), i1, i2)
        return remote(
            fine_ref if own else panel(owner), panel(owner),
            z_send.at[way, k - 1], z_recv.at[way, k - 1], index(i0 + sign, i1, i2),
        )

    def x_copy(a, o1, own=False):
        owner = index(a, i1, i2)
        return remote(
            fine_ref if own else panel(owner), panel(owner),
            gx_send.at[a, o1 - 1], gx_recv.at[a, o1 - 1], index(i0, near(i1, o1, d1), i2),
        )

    def c_copy(a, o1, o2, own=False):
        owner = index(a, near(i1, -o1, d1), i2)
        return remote(
            fine_ref if own else panel(owner), panel(owner),
            gc_send.at[a, o1, o2 - 1], gc_recv.at[a, o1, o2 - 1],
            index(i0, i1, near(i2, o2, d2)),
        )

    def inside(i):
        return (i >= 0) & (i < d0)

    for o1 in range(1, d1):
        x_copy(i0, o1, True).start()
    for way in range(2):
        @pl.when(inside(i0 + 1 - 2 * way))
        def _():
            z_copy(way, 1, True).start()
    for o2 in range(1, d2):
        c_copy(i0, 0, o2, True).start()
    points = []
    for c in range(chunks):
        for d in range(1, n_row):
            to = near(row, d, n_row)
            points.append(remote(
                x_ref.at[pl.ds(pl.multiple_of(to * rows + c * step, step), step), :],
                xbuf.at[row, pl.ds(c * step, step), :],
                x_send.at[d - 1, c], x_recv.at[d - 1, c], to, "row",
            ))
            points[-1].start()

    @pl.loop(0, n_blk)
    def _(g):
        for b in range(blocks):
            hit = named_ref[b, 0] == g
            for j in range(1, names):
                hit = hit | (named_ref[b, j] == g)
            bias[g, :, b * (rows // blocks):(b + 1) * (rows // blocks)] = jnp.full(
                (1, rows // blocks), jnp.where(hit, 0.0, -1e30), F32
            )

    def score(a, o1):
        for o2 in range(1, d2):
            c_copy(a, o1, o2).wait_recv()
        base = pl.multiple_of(index(a, near(i1, -o1, d1), 0) * size, pair)
        whole = panels[pl.ds(base, pair), :].astype(F32)
        norms[pl.ds(base, pair), :] = jnp.broadcast_to(
            jnp.sum(whole * whole, axis=1, keepdims=True), (pair, 128)
        )
        left = panels[pl.ds(base, pair), pl.ds(pl.multiple_of(row * feats, feats), feats)]

        @pl.loop(0, rows // LANES)
        def _(c):
            lane = pl.multiple_of(c * LANES, LANES)
            logits[pl.ds(base, pair), pl.ds(lane, LANES)] = lax.dot_general(
                left, xbuf[row, pl.ds(lane, LANES), :], (((1,), (1,)), ((), ())),
                preferred_element_type=F32,
            )

    def z_event(way, k):
        sign = 1 - 2 * way

        @pl.when(inside(i0 - sign * k))
        def _():
            z_copy(way, k).wait_recv()
            if k < d0 - 1:
                @pl.when(inside(i0 + sign))
                def _():
                    z_copy(way, k + 1).start()
            a = i0 - sign * k
            for o1 in range(1, d1):
                x_copy(a, o1).start()
            for o2 in range(1, d2):
                c_copy(a, 0, o2).start()

    def x_event(a):
        for o1 in range(1, d1):
            x_copy(a, o1).wait_recv()
            for o2 in range(1, d2):
                c_copy(a, o1, o2).start()
        for o1 in range(d1):
            score(a, o1)

    own_x.wait()
    own_panel.wait()
    for k in range(1, d0 + 1):
        if k < d0:
            for way in range(2):
                z_event(way, k)
        if k == 1:
            x_event(i0)
        else:
            for way in range(2):
                a = i0 - (1 - 2 * way) * (k - 1)

                @pl.when(inside(a))
                def _():
                    x_event(a)
    for copy in points:
        copy.wait_recv()

    top[...] = jnp.full(top.shape, -1e30, F32)
    total[...] = jnp.zeros(total.shape, F32)
    scale = 1.0 / (jnp.full((1, LANES), heat_ref[0], F32) * math.sqrt(width))
    tiles = rows // LANES

    @pl.loop(0, n_blk // d2 * tiles)
    def _(t):
        g = lax.div(t, tiles)
        lane = pl.multiple_of(lax.rem(t, tiles) * LANES, LANES)
        lanes = pl.ds(lane, LANES)
        base = pl.multiple_of(g * pair, pair)
        dots = logits[pl.ds(base, pair), lanes]
        for d in range(1, n_row):
            other = near(row, d, n_row)
            dots += lax.dot_general(
                panels[pl.ds(base, pair), pl.ds(pl.multiple_of(other * feats, feats), feats)],
                xbuf[other, lanes, :], (((1,), (1,)), ((), ())),
                preferred_element_type=F32,
            )
        values = []
        old = top[0:1, lanes]
        best = jnp.broadcast_to(old, (8, LANES))
        for j in range(d2):
            norm = norms[pl.ds(base + j * size, size), :1]
            value = (2.0 * dots[j * size:(j + 1) * size] - norm) * scale
            values.append(value + bias[g * d2 + j, :, lanes])
            best = jnp.maximum(best, jnp.max(values[j].reshape(size // 8, 8, LANES), axis=0))
        best = jnp.max(best, axis=0, keepdims=True)
        added = total[:, lanes] * jnp.exp(old - best)
        for j in range(d2):
            value = jnp.exp(values[j] - best)
            logits[pl.ds(base + j * size, size), lanes] = value
            added = added + jnp.sum(value.reshape(size // 8, 8, LANES), axis=0)
        total[:, lanes] = added
        top[:, lanes] = jnp.broadcast_to(best, (8, LANES))
        peaks[g, :, lanes] = best

    summed = jnp.sum(total[...], axis=0, keepdims=True)
    lse_ref[...] = top[0:1, :] + jnp.log(summed)
    total[...] = jnp.broadcast_to(1.0 / summed, total.shape)

    def target(k):
        value = 0
        for z in range(d0):
            far = sorted(range(d0), key=lambda t: (-abs(t - z), t if z >= d0 // 2 else -t))
            value = jnp.where(i0 == z, far[k], value)
        return value

    targets = [target(k) for k in range(d0)]

    def c_sum(k, o1, o2):
        j = near(i2, o2, d2)
        return remote(
            part.at[k * d1 + o1, pl.ds(pl.multiple_of(j * size, size), size), :],
            in_c.at[k * d1 + o1, o2 - 1], c_send.at[k * d1 + o1, o2 - 1],
            c_recv.at[k * d1 + o1, o2 - 1], index(i0, i1, j),
        )

    def b_sum(k, o1, h):
        spot = pl.ds(h * half, half)
        return remote(
            send_b.at[k, o1 - 1, spot, :], in_b.at[k, o1 - 1, spot, :],
            b_send.at[k, o1 - 1, h], b_recv.at[k, o1 - 1, h],
            index(i0, near(i1, o1, d1), i2),
        )

    def a_sum(k, h, way, goal):
        spot = pl.ds(h * half, half)
        return remote(
            send_a.at[min(k, d0 - 2), spot, :], in_a.at[way, goal, spot, :],
            a_send.at[min(k, d0 - 2), h], a_recv.at[way, goal, h],
            index(near(i0, 1 - 2 * way, d0), i1, i2),
        )

    def m_sum(o0, o1, o2):
        to = index(near(i0, o0, d0), near(i1, o1, d1), near(i2, o2, d2))
        return remote(
            mass_out.at[to], mass_in.at[blk], m_send.at[o0, o1, o2], m_recv.at[o0, o1, o2], to
        )

    def weigh(k, o1):
        owner = index(targets[k], near(i1, o1, d1), 0)
        base = pl.multiple_of(owner * size, pair)
        factor = jnp.exp(peaks[lax.div(owner, d2)] - top[0:1, :]) * total[0:1, :]
        weights[...] = (logits[pl.ds(base, pair), :] * factor).astype(BF16)

        @pl.loop(0, n_row)
        def _(s):
            part[k * d1 + o1, :, pl.ds(pl.multiple_of(s * feats, feats), feats)] = jnp.dot(
                weights[...], xbuf[s], preferred_element_type=F32
            ).astype(BF16)

        for o2 in range(1, d2):
            c_sum(k, o1, o2).start()
        mass = lax.dot_general(
            jnp.ones((8, rows), BF16), weights[...], (((1,), (1,)), ((), ())),
            preferred_element_type=F32,
        )
        for j in range(d2):
            mass_out[owner + j] = mass[:, j * size:(j + 1) * size]

    def chip_sum(k, o1, begin, count):
        start = pl.multiple_of(i2 * size + begin, half)
        value = part[k * d1 + o1, pl.ds(start, count), :].astype(F32)
        for o2 in range(1, d2):
            value = value + in_c[k * d1 + o1, o2 - 1, begin:begin + count, :].astype(F32)
        return value

    def ready(k):
        for o1 in range(1, d1):
            for o2 in range(1, d2):
                c_sum(k, o1, o2).wait_recv()
            send_b[k, o1 - 1] = chip_sum(k, o1, 0, size).astype(BF16)

    halves = [(k, h) for k in range(d0) for h in range(2)]

    def pass_on(position):
        if position < len(halves):
            k, h = halves[position]
            for o1 in range(1, d1):
                b_sum(k, o1, h).start()

    started = 0
    for k in range(d0):
        for o1 in range(1, d1):
            weigh(k, o1)
        if k > 0:
            ready(k - 1)
            while started < min(DEPTH, 2 * k):
                pass_on(started)
                started += 1
    weigh(0, 0)
    ready(d0 - 1)
    while started < min(DEPTH, 2 * d0):
        pass_on(started)
        started += 1

    for position, (k, h) in enumerate(halves):
        if h == 0 and k < d0 - 1:
            weigh(k + 1, 0)
            if k == d0 - 2:
                for o0 in range(d0):
                    for o1 in range(d1):
                        for o2 in range(d2):
                            if (o0, o1, o2) != (0, 0, 0):
                                m_sum(o0, o1, o2).start()
        for o1 in range(1, d1):
            b_sum(k, o1, h).wait_recv()
        pass_on(position + DEPTH)
        if h == 0:
            for o2 in range(1, d2):
                c_sum(k, 0, o2).wait_recv()
        value = chip_sum(k, 0, h * half, half)
        for o1 in range(1, d1):
            value = value + in_b[k, o1 - 1, h * half:(h + 1) * half, :].astype(F32)
        spot = pl.ds(h * half, half)
        acc[spot, :] = value
        goal = targets[k]
        if k < d0 - 1:
            way = jnp.where(goal > i0, 0, 1)

            @pl.when(inside(i0 - 1 + 2 * way))
            def _():
                a_sum(k, h, way, goal).wait_recv()
                acc[spot, :] += in_a[way, goal, spot, :].astype(F32)

            send_a[k, spot, :] = acc[spot, :].astype(BF16)
            a_sum(k, h, way, goal).start()

    mass_in[blk] = mass_out[blk]
    mass = None
    for o0 in range(d0):
        for o1 in range(d1):
            for o2 in range(d2):
                if (o0, o1, o2) != (0, 0, 0):
                    m_sum(o0, o1, o2).wait_recv()
    mass = mass_in[0]
    for g in range(1, n_blk):
        mass = mass + mass_in[g]
    column = jnp.broadcast_to(mass[0:1, :], (size, size)).T[:, 0:1] + 1.0
    acc[...] += panels[pl.ds(pl.multiple_of(blk * size, size), size), :].astype(F32)
    for h in range(2):
        spot = pl.ds(h * half, half)
        for way in range(2):
            @pl.when(inside(i0 - 1 + 2 * way))
            def _():
                a_sum(d0 - 1, h, way, i0).wait_recv()
                acc[spot, :] += in_a[way, i0, spot, :].astype(F32)
        out_ref[spot, :] = (acc[spot, :] / column[h * half:(h + 1) * half]).astype(BF16)

    for copy in points:
        copy.wait_send()
    for way in range(2):
        sign = 1 - 2 * way
        for k in range(1, d0):
            @pl.when(inside(i0 + sign) & inside(i0 - sign * (k - 1)))
            def _():
                z_copy(way, k).wait_send()
    for a in range(d0):
        for o1 in range(1, d1):
            x_copy(a, o1).wait_send()
        for o1 in range(d1):
            for o2 in range(1, d2):
                c_copy(a, o1, o2).wait_send()
                c_sum(a, o1, o2).wait_send()
        for h in range(2):
            for o1 in range(1, d1):
                b_sum(a, o1, h).wait_send()
            if a < d0 - 1:
                a_sum(a, h, 0, i0).wait_send()
    for o0 in range(d0):
        for o1 in range(d1):
            for o2 in range(d2):
                if (o0, o1, o2) != (0, 0, 0):
                    m_sum(o0, o1, o2).wait_send()


def shards(n_blk, n_row, coarse, fine, candidates, heat):
    inner = 2 if n_blk < 32 else 4
    dims = (n_blk // (inner * inner), inner, inner)
    d0, d1, d2 = dims
    size, width = fine.shape
    rows = coarse.shape[0] // n_row
    feats = coarse.shape[1]
    vmem = pl.BlockSpec(memory_space=pltpu.VMEM)
    hbm = pl.BlockSpec(memory_space=pl.ANY)
    smem = pl.BlockSpec(memory_space=pltpu.SMEM)
    groups = d0 * d1
    chunks = 4
    dma = pltpu.SemaphoreType.DMA
    new, log_norm = pl.pallas_call(
        functools.partial(kernel, dims, n_row),
        out_shape=(
            jax.ShapeDtypeStruct((size, width), BF16),
            jax.ShapeDtypeStruct((1, rows), F32),
        ),
        in_specs=[hbm, hbm, smem, smem],
        out_specs=(vmem, vmem),
        scratch_shapes=[
            pltpu.VMEM((n_row, rows, feats), BF16),
            pltpu.VMEM((n_blk * size, width), BF16),
            pltpu.VMEM((n_blk * size, rows), F32),
            pltpu.VMEM((n_blk * size, 128), F32),
            pltpu.VMEM((n_blk, 1, rows), F32),
            pltpu.VMEM((8, rows), F32),
            pltpu.VMEM((groups, 1, rows), F32),
            pltpu.VMEM((8, rows), F32),
            pltpu.VMEM((d2 * size, rows), BF16),
            pltpu.VMEM((groups, d2 * size, width), BF16),
            pltpu.VMEM((groups, d2 - 1, size, width), BF16),
            pltpu.VMEM((d0, d1 - 1, size, width), BF16),
            pltpu.VMEM((d0, d1 - 1, size, width), BF16),
            pltpu.VMEM((d0 - 1, size, width), BF16),
            pltpu.VMEM((2, d0, size, width), BF16),
            pltpu.VMEM((size, width), F32),
            pltpu.VMEM((n_blk, 8, size), F32),
            pltpu.VMEM((n_blk, 8, size), F32),
            dma((n_row - 1, chunks)), dma((n_row - 1, chunks)),
            dma((2, d0 - 1)), dma((2, d0 - 1)),
            dma((d0, d1 - 1)), dma((d0, d1 - 1)),
            dma((d0, d1, d2 - 1)), dma((d0, d1, d2 - 1)),
            dma((groups, d2 - 1)), dma((groups, d2 - 1)),
            dma((d0, d1 - 1, 2)), dma((d0, d1 - 1, 2)),
            dma((d0 - 1, 2)), dma((2, d0, 2)),
            dma(dims), dma(dims),
            dma((2,)),
        ],
        compiler_params=pltpu.CompilerParams(
            collective_id=0, has_side_effects=True, vmem_limit_bytes=60 << 20
        ),
        cost_estimate=pl.CostEstimate(
            flops=4 * rows * n_blk * size * width, bytes_accessed=8 << 20,
            transcendentals=rows * n_blk * size,
        ),
    )(coarse, fine, candidates, heat)
    return new, log_norm.reshape(rows)


def solution(mesh):
    return jax.shard_map(
        functools.partial(shards, mesh.shape["blk"], mesh.shape["row"]),
        mesh=mesh,
        in_specs=(P("blk", "row"), P(("blk", "row"), None), P(("blk", "row"), None), P()),
        out_specs=(P(("blk", "row"), None), P(("blk", "row"))),
        check_vma=False,
    )
```

```python
import functools
import math

import jax
import jax.numpy as jnp
from jax import lax
from jax.experimental import pallas as pl
from jax.experimental.pallas import tpu as pltpu
from jax.sharding import PartitionSpec as P

MESH = pl.DeviceIdType.MESH
F32 = jnp.float32
BF16 = jnp.bfloat16
LANES = 256
DEPTH = 3
SPAN = 4


def kernel(
    dims, n_row, x_ref, fine_ref, named_ref, heat_ref, out_ref, lse_ref,
    xbuf, panels, logits, norms, bias, top, peaks, total, weights, part, in_c, send_b, in_b,
    send_a, in_a, acc, mass_out, mass_in,
    x_send, x_recv, z_send, z_recv, gx_send, gx_recv, gc_send, gc_recv, c_send, c_recv,
    b_send, b_recv, a_send, a_recv, m_send, m_recv, own_sem,
):
    d0, d1, d2 = dims
    n_blk = d0 * d1 * d2
    row = lax.axis_index("row")
    blk = lax.axis_index("blk")
    i2 = lax.rem(blk, d2)
    i1 = lax.rem(lax.div(blk, d2), d1)
    i0 = lax.div(blk, d1 * d2)
    size = fine_ref.shape[0]
    width = fine_ref.shape[1]
    rows = xbuf.shape[1]
    feats = xbuf.shape[2]
    pair = d2 * size
    half = size // 2
    chunks = x_send.shape[1]
    step = rows // chunks
    blocks, names = named_ref.shape

    def near(i, o, d):
        return lax.rem(i + o + d, d)

    def index(a, b, c):
        return (a * d1 + b) * d2 + c

    def panel(owner):
        return panels.at[pl.ds(pl.multiple_of(owner * size, size), size), :]

    def remote(src, dst, send, recv, to, axis="blk"):
        return pltpu.make_async_remote_copy(
            src_ref=src, dst_ref=dst, send_sem=send, recv_sem=recv,
            device_id={axis: to}, device_id_type=MESH,
        )

    barrier = pltpu.get_barrier_semaphore()
    for d in range(1, n_row):
        pl.semaphore_signal(
            barrier, inc=1, device_id={"row": near(row, d, n_row)}, device_id_type=MESH
        )
    for d in range(1, n_blk):
        pl.semaphore_signal(
            barrier, inc=1, device_id={"blk": near(blk, d, n_blk)}, device_id_type=MESH
        )
    own_x = pltpu.make_async_copy(
        x_ref.at[pl.ds(pl.multiple_of(row * rows, rows), rows), :], xbuf.at[row], own_sem.at[0]
    )
    own_x.start()
    own_panel = pltpu.make_async_copy(fine_ref, panel(blk), own_sem.at[1])
    own_panel.start()
    pl.semaphore_wait(barrier, n_row - 1 + n_blk - 1)

    def z_copy(way, k, own=False):
        sign = 1 - 2 * way
        owner = index(i0 - sign * (k - 1), i1, i2)
        return remote(
            fine_ref if own else panel(owner), panel(owner),
            z_send.at[way, k - 1], z_recv.at[way, k - 1], index(i0 + sign, i1, i2),
        )

    def x_copy(a, o1, own=False):
        owner = index(a, i1, i2)
        return remote(
            fine_ref if own else panel(owner), panel(owner),
            gx_send.at[a, o1 - 1], gx_recv.at[a, o1 - 1], index(i0, near(i1, o1, d1), i2),
        )

    def c_copy(a, o1, o2, own=False):
        owner = index(a, near(i1, -o1, d1), i2)
        return remote(
            fine_ref if own else panel(owner), panel(owner),
            gc_send.at[a, o1, o2 - 1], gc_recv.at[a, o1, o2 - 1],
            index(i0, i1, near(i2, o2, d2)),
        )

    def inside(i):
        return (i >= 0) & (i < d0)

    for o1 in range(1, d1):
        x_copy(i0, o1, True).start()
    for way in range(2):
        @pl.when(inside(i0 + 1 - 2 * way))
        def _():
            z_copy(way, 1, True).start()
    for o2 in range(1, d2):
        c_copy(i0, 0, o2, True).start()
    points = []
    for c in range(chunks):
        for d in range(1, n_row):
            to = near(row, d, n_row)
            points.append(remote(
                x_ref.at[pl.ds(pl.multiple_of(to * rows + c * step, step), step), :],
                xbuf.at[row, pl.ds(c * step, step), :],
                x_send.at[d - 1, c], x_recv.at[d - 1, c], to, "row",
            ))
            points[-1].start()

    @pl.loop(0, n_blk)
    def _(g):
        for b in range(blocks):
            hit = named_ref[b, 0] == g
            for j in range(1, names):
                hit = hit | (named_ref[b, j] == g)
            bias[g, :, b * (rows // blocks):(b + 1) * (rows // blocks)] = jnp.full(
                (1, rows // blocks), jnp.where(hit, 0.0, -1e30), F32
            )

    scale = 1.0 / (jnp.full((1, LANES), heat_ref[0], F32) * math.sqrt(width))
    top[...] = jnp.full(top.shape, -1e30, F32)
    total[...] = jnp.zeros(total.shape, F32)

    def score(a, o1):
        for o2 in range(1, d2):
            c_copy(a, o1, o2).wait_recv()
        base = pl.multiple_of(index(a, near(i1, -o1, d1), 0) * size, pair)
        whole = panels[pl.ds(base, pair), :].astype(F32)
        norms[pl.ds(base, pair), :] = jnp.broadcast_to(
            jnp.sum(whole * whole, axis=1, keepdims=True), (pair, 128)
        ) * scale[:, :128]
        left = panels[pl.ds(base, pair), pl.ds(pl.multiple_of(row * feats, feats), feats)]

        @pl.loop(0, rows // LANES)
        def _(c):
            lane = pl.multiple_of(c * LANES, LANES)
            logits[pl.ds(base, pair), pl.ds(lane, LANES)] = lax.dot_general(
                left, xbuf[row, pl.ds(lane, LANES), :], (((1,), (1,)), ((), ())),
                preferred_element_type=F32,
            )

    def z_event(way, k):
        sign = 1 - 2 * way

        @pl.when(inside(i0 - sign * k))
        def _():
            z_copy(way, k).wait_recv()
            if k < d0 - 1:
                @pl.when(inside(i0 + sign))
                def _():
                    z_copy(way, k + 1).start()
            a = i0 - sign * k
            for o1 in range(1, d1):
                x_copy(a, o1).start()
            for o2 in range(1, d2):
                c_copy(a, 0, o2).start()

    def x_event(a):
        for o1 in range(1, d1):
            x_copy(a, o1).wait_recv()
            for o2 in range(1, d2):
                c_copy(a, o1, o2).start()
        for o1 in range(d1):
            score(a, o1)

    spans = n_blk // SPAN

    def fuse(g, c):
        lanes = pl.ds(c * LANES, LANES)
        base = pl.multiple_of(g * (SPAN * size), SPAN * size)
        tile = pl.ds(base, SPAN * size)
        dots = logits[tile, lanes]
        for d in range(1, n_row):
            other = near(row, d, n_row)
            dots += lax.dot_general(
                panels[tile, pl.ds(pl.multiple_of(other * feats, feats), feats)],
                xbuf[other, lanes, :], (((1,), (1,)), ((), ())),
                preferred_element_type=F32,
            )
        values = []
        old = top[0:1, lanes]
        best = jnp.broadcast_to(old, (8, LANES))
        for j in range(SPAN):
            norm = norms[pl.ds(base + j * size, size), :1]
            value = dots[j * size:(j + 1) * size] * (2.0 * scale) - norm
            values.append(value + bias[g * SPAN + j, :, lanes])
            best = jnp.maximum(best, jnp.max(values[j].reshape(size // 8, 8, LANES), axis=0))
        best = jnp.max(best, axis=0, keepdims=True)
        added = total[:, lanes] * jnp.exp(old - best)
        for j in range(SPAN):
            value = jnp.exp(values[j] - best)
            logits[pl.ds(base + j * size, size), lanes] = value
            added = added + jnp.sum(value.reshape(size // 8, 8, LANES), axis=0)
        total[:, lanes] = added
        top[:, lanes] = jnp.broadcast_to(best, (8, LANES))
        peaks[g, :, lanes] = best

    own_x.wait()
    own_panel.wait()
    late = jnp.where(i0 < d0 // 2, d0 - 1, 0)
    for k in range(1, d0):
        for way in range(2):
            z_event(way, k)
        if k == 1:
            x_event(i0)
        else:
            for way in range(2):
                a = i0 - (1 - 2 * way) * (k - 1)

                @pl.when(inside(a) & (a != late))
                def _():
                    x_event(a)

    each = d1 * d2 // SPAN
    first = jnp.where(late == 0, each, 0)
    for c in range(chunks):
        for copy in points[c * (n_row - 1):(c + 1) * (n_row - 1)]:
            copy.wait_recv()

        @pl.loop(0, spans - each)
        def _(g):
            fuse(first + g, c)

    x_event(late)
    for c in range(chunks):
        @pl.loop(0, each)
        def _(g):
            fuse(late * each + g, c)

    summed = jnp.sum(total[...], axis=0, keepdims=True)
    lse_ref[...] = top[0:1, :] + jnp.log(summed)
    total[...] = jnp.broadcast_to(1.0 / summed, total.shape)

    def target(k):
        value = 0
        for z in range(d0):
            far = sorted(range(d0), key=lambda t: (-abs(t - z), t if z >= d0 // 2 else -t))
            value = jnp.where(i0 == z, far[k], value)
        return value

    targets = [target(k) for k in range(d0)]

    def c_sum(k, o1, o2):
        j = near(i2, o2, d2)
        return remote(
            part.at[k * d1 + o1, pl.ds(pl.multiple_of(j * size, size), size), :],
            in_c.at[k * d1 + o1, o2 - 1], c_send.at[k * d1 + o1, o2 - 1],
            c_recv.at[k * d1 + o1, o2 - 1], index(i0, i1, j),
        )

    def b_sum(k, o1, h):
        spot = pl.ds(h * half, half)
        return remote(
            send_b.at[k, o1 - 1, spot, :], in_b.at[k, o1 - 1, spot, :],
            b_send.at[k, o1 - 1, h], b_recv.at[k, o1 - 1, h],
            index(i0, near(i1, o1, d1), i2),
        )

    def a_sum(k, h, way, goal):
        spot = pl.ds(h * half, half)
        return remote(
            send_a.at[min(k, d0 - 2), spot, :], in_a.at[way, goal, spot, :],
            a_send.at[min(k, d0 - 2), h], a_recv.at[way, goal, h],
            index(near(i0, 1 - 2 * way, d0), i1, i2),
        )

    def m_sum(o0, o1, o2):
        to = index(near(i0, o0, d0), near(i1, o1, d1), near(i2, o2, d2))
        return remote(
            mass_out.at[to], mass_in.at[blk], m_send.at[o0, o1, o2], m_recv.at[o0, o1, o2], to
        )

    def weigh(k, o1):
        owner = index(targets[k], near(i1, o1, d1), 0)
        base = pl.multiple_of(owner * size, pair)
        factor = jnp.exp(peaks[lax.div(owner, SPAN)] - top[0:1, :]) * total[0:1, :]
        weights[...] = (logits[pl.ds(base, pair), :] * factor).astype(BF16)

        @pl.loop(0, n_row)
        def _(s):
            part[k * d1 + o1, :, pl.ds(pl.multiple_of(s * feats, feats), feats)] = jnp.dot(
                weights[...], xbuf[s], preferred_element_type=F32
            ).astype(BF16)

        for o2 in range(1, d2):
            c_sum(k, o1, o2).start()
        mass = lax.dot_general(
            jnp.ones((8, rows), BF16), weights[...], (((1,), (1,)), ((), ())),
            preferred_element_type=F32,
        )
        for j in range(d2):
            mass_out[owner + j] = mass[:, j * size:(j + 1) * size]

    def chip_sum(k, o1, begin, count):
        start = pl.multiple_of(i2 * size + begin, half)
        value = part[k * d1 + o1, pl.ds(start, count), :].astype(F32)
        for o2 in range(1, d2):
            value = value + in_c[k * d1 + o1, o2 - 1, begin:begin + count, :].astype(F32)
        return value

    def ready(k):
        for o1 in range(1, d1):
            for o2 in range(1, d2):
                c_sum(k, o1, o2).wait_recv()
            send_b[k, o1 - 1] = chip_sum(k, o1, 0, size).astype(BF16)

    halves = [(k, h) for k in range(d0) for h in range(2)]

    def pass_on(position):
        if position < len(halves):
            k, h = halves[position]
            for o1 in range(1, d1):
                b_sum(k, o1, h).start()

    started = 0
    for k in range(d0):
        for o1 in range(1, d1):
            weigh(k, o1)
        if k > 0:
            ready(k - 1)
            while started < min(DEPTH, 2 * k):
                pass_on(started)
                started += 1
    weigh(0, 0)
    ready(d0 - 1)
    while started < min(DEPTH, 2 * d0):
        pass_on(started)
        started += 1

    for position, (k, h) in enumerate(halves):
        if h == 0 and k < d0 - 1:
            weigh(k + 1, 0)
            if k == d0 - 2:
                for o0 in range(d0):
                    for o1 in range(d1):
                        for o2 in range(d2):
                            if (o0, o1, o2) != (0, 0, 0):
                                m_sum(o0, o1, o2).start()
        for o1 in range(1, d1):
            b_sum(k, o1, h).wait_recv()
        pass_on(position + DEPTH)
        if h == 0:
            for o2 in range(1, d2):
                c_sum(k, 0, o2).wait_recv()
        value = chip_sum(k, 0, h * half, half)
        for o1 in range(1, d1):
            value = value + in_b[k, o1 - 1, h * half:(h + 1) * half, :].astype(F32)
        spot = pl.ds(h * half, half)
        acc[spot, :] = value
        goal = targets[k]
        if k < d0 - 1:
            way = jnp.where(goal > i0, 0, 1)

            @pl.when(inside(i0 - 1 + 2 * way))
            def _():
                a_sum(k, h, way, goal).wait_recv()
                acc[spot, :] += in_a[way, goal, spot, :].astype(F32)

            send_a[k, spot, :] = acc[spot, :].astype(BF16)
            a_sum(k, h, way, goal).start()

    mass_in[blk] = mass_out[blk]
    mass = None
    for o0 in range(d0):
        for o1 in range(d1):
            for o2 in range(d2):
                if (o0, o1, o2) != (0, 0, 0):
                    m_sum(o0, o1, o2).wait_recv()
    mass = mass_in[0]
    for g in range(1, n_blk):
        mass = mass + mass_in[g]
    column = jnp.broadcast_to(mass[0:1, :], (size, size)).T[:, 0:1] + 1.0
    acc[...] += panels[pl.ds(pl.multiple_of(blk * size, size), size), :].astype(F32)
    for h in range(2):
        spot = pl.ds(h * half, half)
        for way in range(2):
            @pl.when(inside(i0 - 1 + 2 * way))
            def _():
                a_sum(d0 - 1, h, way, i0).wait_recv()
                acc[spot, :] += in_a[way, i0, spot, :].astype(F32)
        out_ref[spot, :] = (acc[spot, :] / column[h * half:(h + 1) * half]).astype(BF16)

    for copy in points:
        copy.wait_send()
    for way in range(2):
        sign = 1 - 2 * way
        for k in range(1, d0):
            @pl.when(inside(i0 + sign) & inside(i0 - sign * (k - 1)))
            def _():
                z_copy(way, k).wait_send()
    for a in range(d0):
        for o1 in range(1, d1):
            x_copy(a, o1).wait_send()
        for o1 in range(d1):
            for o2 in range(1, d2):
                c_copy(a, o1, o2).wait_send()
                c_sum(a, o1, o2).wait_send()
        for h in range(2):
            for o1 in range(1, d1):
                b_sum(a, o1, h).wait_send()
            if a < d0 - 1:
                a_sum(a, h, 0, i0).wait_send()
    for o0 in range(d0):
        for o1 in range(d1):
            for o2 in range(d2):
                if (o0, o1, o2) != (0, 0, 0):
                    m_sum(o0, o1, o2).wait_send()


def shards(n_blk, n_row, coarse, fine, candidates, heat):
    inner = 2 if n_blk < 32 else 4
    dims = (n_blk // (inner * inner), inner, inner)
    d0, d1, d2 = dims
    size, width = fine.shape
    rows = coarse.shape[0] // n_row
    feats = coarse.shape[1]
    vmem = pl.BlockSpec(memory_space=pltpu.VMEM)
    hbm = pl.BlockSpec(memory_space=pl.ANY)
    smem = pl.BlockSpec(memory_space=pltpu.SMEM)
    groups = d0 * d1
    chunks = rows // LANES
    dma = pltpu.SemaphoreType.DMA
    new, log_norm = pl.pallas_call(
        functools.partial(kernel, dims, n_row),
        out_shape=(
            jax.ShapeDtypeStruct((size, width), BF16),
            jax.ShapeDtypeStruct((1, rows), F32),
        ),
        in_specs=[hbm, hbm, smem, smem],
        out_specs=(vmem, vmem),
        scratch_shapes=[
            pltpu.VMEM((n_row, rows, feats), BF16),
            pltpu.VMEM((n_blk * size, width), BF16),
            pltpu.VMEM((n_blk * size, rows), F32),
            pltpu.VMEM((n_blk * size, 128), F32),
            pltpu.VMEM((n_blk, 1, rows), F32),
            pltpu.VMEM((8, rows), F32),
            pltpu.VMEM((n_blk // SPAN, 1, rows), F32),
            pltpu.VMEM((8, rows), F32),
            pltpu.VMEM((d2 * size, rows), BF16),
            pltpu.VMEM((groups, d2 * size, width), BF16),
            pltpu.VMEM((groups, d2 - 1, size, width), BF16),
            pltpu.VMEM((d0, d1 - 1, size, width), BF16),
            pltpu.VMEM((d0, d1 - 1, size, width), BF16),
            pltpu.VMEM((d0 - 1, size, width), BF16),
            pltpu.VMEM((2, d0, size, width), BF16),
            pltpu.VMEM((size, width), F32),
            pltpu.VMEM((n_blk, 8, size), F32),
            pltpu.VMEM((n_blk, 8, size), F32),
            dma((n_row - 1, chunks)), dma((n_row - 1, chunks)),
            dma((2, d0 - 1)), dma((2, d0 - 1)),
            dma((d0, d1 - 1)), dma((d0, d1 - 1)),
            dma((d0, d1, d2 - 1)), dma((d0, d1, d2 - 1)),
            dma((groups, d2 - 1)), dma((groups, d2 - 1)),
            dma((d0, d1 - 1, 2)), dma((d0, d1 - 1, 2)),
            dma((d0 - 1, 2)), dma((2, d0, 2)),
            dma(dims), dma(dims),
            dma((2,)),
        ],
        compiler_params=pltpu.CompilerParams(
            collective_id=0, has_side_effects=True, vmem_limit_bytes=60 << 20
        ),
        cost_estimate=pl.CostEstimate(
            flops=4 * rows * n_blk * size * width, bytes_accessed=8 << 20,
            transcendentals=rows * n_blk * size,
        ),
    )(coarse, fine, candidates, heat)
    return new, log_norm.reshape(rows)


def solution(mesh):
    return jax.shard_map(
        functools.partial(shards, mesh.shape["blk"], mesh.shape["row"]),
        mesh=mesh,
        in_specs=(P("blk", "row"), P(("blk", "row"), None), P(("blk", "row"), None), P()),
        out_specs=(P(("blk", "row"), None), P(("blk", "row"))),
        check_vma=False,
    )
```

```python
import functools
import math

import jax
import jax.numpy as jnp
from jax import lax
from jax.experimental import pallas as pl
from jax.experimental.pallas import tpu as pltpu
from jax.sharding import PartitionSpec as P

MESH = pl.DeviceIdType.MESH
F32 = jnp.float32
BF16 = jnp.bfloat16
LANES = 256
DEPTH = 3
SPAN = 4


def kernel(
    dims, n_row, x_ref, fine_ref, named_ref, heat_ref, out_ref, lse_ref,
    xbuf, panels, logits, norms, bias, top, peaks, total, weights, part, in_c, send_b, in_b,
    send_a, in_a, acc, mass_out, mass_in,
    x_send, x_recv, z_send, z_recv, gx_send, gx_recv, gc_send, gc_recv, c_send, c_recv,
    b_send, b_recv, a_send, a_recv, m_send, m_recv, own_sem,
):
    d0, d1, d2 = dims
    n_blk = d0 * d1 * d2
    row = lax.axis_index("row")
    blk = lax.axis_index("blk")
    i2 = lax.rem(blk, d2)
    i1 = lax.rem(lax.div(blk, d2), d1)
    i0 = lax.div(blk, d1 * d2)
    size = fine_ref.shape[0]
    width = fine_ref.shape[1]
    rows = xbuf.shape[1]
    feats = xbuf.shape[2]
    pair = d2 * size
    half = size // 2
    chunks = x_send.shape[1]
    step = rows // chunks
    blocks, names = named_ref.shape

    def near(i, o, d):
        return lax.rem(i + o + d, d)

    def index(a, b, c):
        return (a * d1 + b) * d2 + c

    def panel(owner):
        return panels.at[pl.ds(pl.multiple_of(owner * size, size), size), :]

    def remote(src, dst, send, recv, to, axis="blk"):
        return pltpu.make_async_remote_copy(
            src_ref=src, dst_ref=dst, send_sem=send, recv_sem=recv,
            device_id={axis: to}, device_id_type=MESH,
        )

    barrier = pltpu.get_barrier_semaphore()
    for d in range(1, n_row):
        pl.semaphore_signal(
            barrier, inc=1, device_id={"row": near(row, d, n_row)}, device_id_type=MESH
        )
    for d in range(1, n_blk):
        pl.semaphore_signal(
            barrier, inc=1, device_id={"blk": near(blk, d, n_blk)}, device_id_type=MESH
        )
    own_x = pltpu.make_async_copy(
        x_ref.at[pl.ds(pl.multiple_of(row * rows, rows), rows), :], xbuf.at[row], own_sem.at[0]
    )
    own_x.start()
    own_panel = pltpu.make_async_copy(fine_ref, panel(blk), own_sem.at[1])
    own_panel.start()
    pl.semaphore_wait(barrier, n_row - 1 + n_blk - 1)

    def z_copy(way, k, own=False):
        sign = 1 - 2 * way
        owner = index(i0 - sign * (k - 1), i1, i2)
        return remote(
            fine_ref if own else panel(owner), panel(owner),
            z_send.at[way, k - 1], z_recv.at[way, k - 1], index(i0 + sign, i1, i2),
        )

    def x_copy(a, o1, own=False):
        owner = index(a, i1, i2)
        return remote(
            fine_ref if own else panel(owner), panel(owner),
            gx_send.at[a, o1 - 1], gx_recv.at[a, o1 - 1], index(i0, near(i1, o1, d1), i2),
        )

    def c_copy(a, o1, o2, own=False):
        owner = index(a, near(i1, -o1, d1), i2)
        return remote(
            fine_ref if own else panel(owner), panel(owner),
            gc_send.at[a, o1, o2 - 1], gc_recv.at[a, o1, o2 - 1],
            index(i0, i1, near(i2, o2, d2)),
        )

    def inside(i):
        return (i >= 0) & (i < d0)

    for o1 in range(1, d1):
        x_copy(i0, o1, True).start()
    for way in range(2):
        @pl.when(inside(i0 + 1 - 2 * way))
        def _():
            z_copy(way, 1, True).start()
    for o2 in range(1, d2):
        c_copy(i0, 0, o2, True).start()
    points = []
    for c in range(chunks):
        for d in range(1, n_row):
            to = near(row, d, n_row)
            points.append(remote(
                x_ref.at[pl.ds(pl.multiple_of(to * rows + c * step, step), step), :],
                xbuf.at[row, pl.ds(c * step, step), :],
                x_send.at[d - 1, c], x_recv.at[d - 1, c], to, "row",
            ))

    def send_points(c):
        for copy in points[c * (n_row - 1):(c + 1) * (n_row - 1)]:
            copy.start()

    for c in range(min(2, chunks)):
        send_points(c)

    @pl.loop(0, n_blk)
    def _(g):
        for b in range(blocks):
            hit = named_ref[b, 0] == g
            for j in range(1, names):
                hit = hit | (named_ref[b, j] == g)
            bias[g, :, b * (rows // blocks):(b + 1) * (rows // blocks)] = jnp.full(
                (1, rows // blocks), jnp.where(hit, 0.0, -1e30), F32
            )

    scale = 1.0 / (jnp.full((1, LANES), heat_ref[0], F32) * math.sqrt(width))
    top[...] = jnp.full(top.shape, -1e30, F32)
    total[...] = jnp.zeros(total.shape, F32)

    def measure(a, o1):
        for o2 in range(1, d2):
            c_copy(a, o1, o2).wait_recv()
        base = pl.multiple_of(index(a, near(i1, -o1, d1), 0) * size, pair)
        whole = panels[pl.ds(base, pair), :].astype(F32)
        norms[pl.ds(base, pair), :] = jnp.broadcast_to(
            jnp.sum(whole * whole, axis=1, keepdims=True), (pair, 128)
        ) * scale[:, :128]
        return base

    def score(a, o1):
        base = measure(a, o1)
        left = panels[pl.ds(base, pair), pl.ds(pl.multiple_of(row * feats, feats), feats)]

        @pl.loop(0, rows // LANES)
        def _(c):
            lane = pl.multiple_of(c * LANES, LANES)
            logits[pl.ds(base, pair), pl.ds(lane, LANES)] = lax.dot_general(
                left, xbuf[row, pl.ds(lane, LANES), :], (((1,), (1,)), ((), ())),
                preferred_element_type=F32,
            )

    def z_event(way, k):
        sign = 1 - 2 * way

        @pl.when(inside(i0 - sign * k))
        def _():
            z_copy(way, k).wait_recv()
            if k < d0 - 1:
                @pl.when(inside(i0 + sign))
                def _():
                    z_copy(way, k + 1).start()
            a = i0 - sign * k
            for o1 in range(1, d1):
                x_copy(a, o1).start()
            for o2 in range(1, d2):
                c_copy(a, 0, o2).start()

    def x_arrival(a):
        for o1 in range(1, d1):
            x_copy(a, o1).wait_recv()
            for o2 in range(1, d2):
                c_copy(a, o1, o2).start()

    def x_event(a):
        x_arrival(a)
        for o1 in range(d1):
            score(a, o1)

    joint = max(1, min(d1, SPAN // d2))

    def fuse(g, c, count, full=False):
        lanes = pl.ds(c * LANES, LANES)
        base = pl.multiple_of(g * pair, pair)
        tile = pl.ds(base, count * pair)
        dots = None if full else logits[tile, lanes]
        for d in range(0 if full else 1, n_row):
            other = near(row, d, n_row)
            term = lax.dot_general(
                panels[tile, pl.ds(pl.multiple_of(other * feats, feats), feats)],
                xbuf[other, lanes, :], (((1,), (1,)), ((), ())),
                preferred_element_type=F32,
            )
            dots = term if dots is None else dots + term
        values = []
        old = top[0:1, lanes]
        best = jnp.broadcast_to(old, (8, LANES))
        for j in range(count * d2):
            norm = norms[pl.ds(base + j * size, size), :1]
            value = dots[j * size:(j + 1) * size] * (2.0 * scale) - norm
            values.append(value + bias[g * d2 + j, :, lanes])
            best = jnp.maximum(best, jnp.max(values[j].reshape(size // 8, 8, LANES), axis=0))
        best = jnp.max(best, axis=0, keepdims=True)
        added = total[:, lanes] * jnp.exp(old - best)
        for j in range(count * d2):
            value = jnp.exp(values[j] - best)
            logits[pl.ds(base + j * size, size), lanes] = value
            added = added + jnp.sum(value.reshape(size // 8, 8, LANES), axis=0)
        total[:, lanes] = added
        top[:, lanes] = jnp.broadcast_to(best, (8, LANES))
        for j in range(count):
            peaks[g + j, :, lanes] = best

    own_x.wait()
    own_panel.wait()
    late = jnp.where(i0 < d0 // 2, d0 - 1, 0)
    for k in range(1, d0):
        for way in range(2):
            z_event(way, k)
        if k == 1:
            x_event(i0)
        else:
            for way in range(2):
                a = i0 - (1 - 2 * way) * (k - 1)

                @pl.when(inside(a) & (a != late))
                def _():
                    x_event(a)
        if k + 1 < chunks:
            send_points(k + 1)
    for c in range(max(2, d0 + 1), chunks):
        send_points(c)
    score(late, 0)

    each = d1 // joint
    first = jnp.where(late == 0, d1, 0)
    for c in range(chunks):
        if c == chunks - 1:
            x_arrival(late)
        for copy in points[c * (n_row - 1):(c + 1) * (n_row - 1)]:
            copy.wait_recv()
        fuse(late * d1 + i1, c, 1)

        @pl.loop(0, (d0 - 1) * each)
        def _(g):
            fuse(first + g * joint, c, joint)

    for o1 in range(1, d1):
        measure(late, o1)
        g = late * d1 + near(i1, -o1, d1)
        for c in range(chunks):
            fuse(g, c, 1, True)

    summed = jnp.sum(total[...], axis=0, keepdims=True)
    lse_ref[...] = top[0:1, :] + jnp.log(summed)
    total[...] = jnp.broadcast_to(1.0 / summed, total.shape)

    def target(k):
        value = 0
        for z in range(d0):
            far = sorted(range(d0), key=lambda t: (-abs(t - z), t if z >= d0 // 2 else -t))
            value = jnp.where(i0 == z, far[k], value)
        return value

    targets = [target(k) for k in range(d0)]

    def c_sum(k, o1, o2):
        j = near(i2, o2, d2)
        return remote(
            part.at[k * d1 + o1, pl.ds(pl.multiple_of(j * size, size), size), :],
            in_c.at[k * d1 + o1, o2 - 1], c_send.at[k * d1 + o1, o2 - 1],
            c_recv.at[k * d1 + o1, o2 - 1], index(i0, i1, j),
        )

    def b_sum(k, o1, h):
        spot = pl.ds(h * half, half)
        return remote(
            send_b.at[k, o1 - 1, spot, :], in_b.at[k, o1 - 1, spot, :],
            b_send.at[k, o1 - 1, h], b_recv.at[k, o1 - 1, h],
            index(i0, near(i1, o1, d1), i2),
        )

    def a_sum(k, h, way, goal):
        spot = pl.ds(h * half, half)
        return remote(
            send_a.at[min(k, d0 - 2), spot, :], in_a.at[way, goal, spot, :],
            a_send.at[min(k, d0 - 2), h], a_recv.at[way, goal, h],
            index(near(i0, 1 - 2 * way, d0), i1, i2),
        )

    def m_sum(o0, o1, o2):
        to = index(near(i0, o0, d0), near(i1, o1, d1), near(i2, o2, d2))
        return remote(
            mass_out.at[to], mass_in.at[blk], m_send.at[o0, o1, o2], m_recv.at[o0, o1, o2], to
        )

    def weigh(k, o1):
        owner = index(targets[k], near(i1, o1, d1), 0)
        base = pl.multiple_of(owner * size, pair)
        factor = jnp.exp(peaks[lax.div(owner, d2)] - top[0:1, :]) * total[0:1, :]
        weights[...] = (logits[pl.ds(base, pair), :] * factor).astype(BF16)

        @pl.loop(0, n_row)
        def _(s):
            part[k * d1 + o1, :, pl.ds(pl.multiple_of(s * feats, feats), feats)] = jnp.dot(
                weights[...], xbuf[s], preferred_element_type=F32
            ).astype(BF16)

        for o2 in range(1, d2):
            c_sum(k, o1, o2).start()
        mass = lax.dot_general(
            jnp.ones((8, rows), BF16), weights[...], (((1,), (1,)), ((), ())),
            preferred_element_type=F32,
        )
        for j in range(d2):
            mass_out[owner + j] = mass[:, j * size:(j + 1) * size]

    def chip_sum(k, o1, begin, count):
        start = pl.multiple_of(i2 * size + begin, half)
        value = part[k * d1 + o1, pl.ds(start, count), :].astype(F32)
        for o2 in range(1, d2):
            value = value + in_c[k * d1 + o1, o2 - 1, begin:begin + count, :].astype(F32)
        return value

    def ready(k):
        for o1 in range(1, d1):
            for o2 in range(1, d2):
                c_sum(k, o1, o2).wait_recv()
            send_b[k, o1 - 1] = chip_sum(k, o1, 0, size).astype(BF16)

    halves = [(k, h) for k in range(d0) for h in range(2)]

    def pass_on(position):
        if position < len(halves):
            k, h = halves[position]
            for o1 in range(1, d1):
                b_sum(k, o1, h).start()

    started = 0
    for k in range(d0):
        for o1 in range(1, d1):
            weigh(k, o1)
        if k > 0:
            ready(k - 1)
            while started < min(DEPTH, 2 * k):
                pass_on(started)
                started += 1
    weigh(0, 0)
    ready(d0 - 1)
    while started < min(DEPTH, 2 * d0):
        pass_on(started)
        started += 1

    for position, (k, h) in enumerate(halves):
        if h == 0 and k < d0 - 1:
            weigh(k + 1, 0)
            if k == d0 - 2:
                for o0 in range(d0):
                    for o1 in range(d1):
                        for o2 in range(d2):
                            if (o0, o1, o2) != (0, 0, 0):
                                m_sum(o0, o1, o2).start()
        for o1 in range(1, d1):
            b_sum(k, o1, h).wait_recv()
        pass_on(position + DEPTH)
        if h == 0:
            for o2 in range(1, d2):
                c_sum(k, 0, o2).wait_recv()
        value = chip_sum(k, 0, h * half, half)
        for o1 in range(1, d1):
            value = value + in_b[k, o1 - 1, h * half:(h + 1) * half, :].astype(F32)
        spot = pl.ds(h * half, half)
        acc[spot, :] = value
        goal = targets[k]
        if k < d0 - 1:
            way = jnp.where(goal > i0, 0, 1)

            @pl.when(inside(i0 - 1 + 2 * way))
            def _():
                a_sum(k, h, way, goal).wait_recv()
                acc[spot, :] += in_a[way, goal, spot, :].astype(F32)

            send_a[k, spot, :] = acc[spot, :].astype(BF16)
            a_sum(k, h, way, goal).start()

    mass_in[blk] = mass_out[blk]
    mass = None
    for o0 in range(d0):
        for o1 in range(d1):
            for o2 in range(d2):
                if (o0, o1, o2) != (0, 0, 0):
                    m_sum(o0, o1, o2).wait_recv()
    mass = mass_in[0]
    for g in range(1, n_blk):
        mass = mass + mass_in[g]
    column = jnp.broadcast_to(mass[0:1, :], (size, size)).T[:, 0:1] + 1.0
    acc[...] += panels[pl.ds(pl.multiple_of(blk * size, size), size), :].astype(F32)
    for h in range(2):
        spot = pl.ds(h * half, half)
        for way in range(2):
            @pl.when(inside(i0 - 1 + 2 * way))
            def _():
                a_sum(d0 - 1, h, way, i0).wait_recv()
                acc[spot, :] += in_a[way, i0, spot, :].astype(F32)
        out_ref[spot, :] = (acc[spot, :] / column[h * half:(h + 1) * half]).astype(BF16)

    for copy in points:
        copy.wait_send()
    for way in range(2):
        sign = 1 - 2 * way
        for k in range(1, d0):
            @pl.when(inside(i0 + sign) & inside(i0 - sign * (k - 1)))
            def _():
                z_copy(way, k).wait_send()
    for a in range(d0):
        for o1 in range(1, d1):
            x_copy(a, o1).wait_send()
        for o1 in range(d1):
            for o2 in range(1, d2):
                c_copy(a, o1, o2).wait_send()
                c_sum(a, o1, o2).wait_send()
        for h in range(2):
            for o1 in range(1, d1):
                b_sum(a, o1, h).wait_send()
            if a < d0 - 1:
                a_sum(a, h, 0, i0).wait_send()
    for o0 in range(d0):
        for o1 in range(d1):
            for o2 in range(d2):
                if (o0, o1, o2) != (0, 0, 0):
                    m_sum(o0, o1, o2).wait_send()


def shards(n_blk, n_row, coarse, fine, candidates, heat):
    inner = 2 if n_blk < 32 else 4
    dims = (n_blk // (inner * inner), inner, inner)
    d0, d1, d2 = dims
    size, width = fine.shape
    rows = coarse.shape[0] // n_row
    feats = coarse.shape[1]
    vmem = pl.BlockSpec(memory_space=pltpu.VMEM)
    hbm = pl.BlockSpec(memory_space=pl.ANY)
    smem = pl.BlockSpec(memory_space=pltpu.SMEM)
    groups = d0 * d1
    chunks = rows // LANES
    dma = pltpu.SemaphoreType.DMA
    new, log_norm = pl.pallas_call(
        functools.partial(kernel, dims, n_row),
        out_shape=(
            jax.ShapeDtypeStruct((size, width), BF16),
            jax.ShapeDtypeStruct((1, rows), F32),
        ),
        in_specs=[hbm, hbm, smem, smem],
        out_specs=(vmem, vmem),
        scratch_shapes=[
            pltpu.VMEM((n_row, rows, feats), BF16),
            pltpu.VMEM((n_blk * size, width), BF16),
            pltpu.VMEM((n_blk * size, rows), F32),
            pltpu.VMEM((n_blk * size, 128), F32),
            pltpu.VMEM((n_blk, 1, rows), F32),
            pltpu.VMEM((8, rows), F32),
            pltpu.VMEM((groups, 1, rows), F32),
            pltpu.VMEM((8, rows), F32),
            pltpu.VMEM((d2 * size, rows), BF16),
            pltpu.VMEM((groups, d2 * size, width), BF16),
            pltpu.VMEM((groups, d2 - 1, size, width), BF16),
            pltpu.VMEM((d0, d1 - 1, size, width), BF16),
            pltpu.VMEM((d0, d1 - 1, size, width), BF16),
            pltpu.VMEM((d0 - 1, size, width), BF16),
            pltpu.VMEM((2, d0, size, width), BF16),
            pltpu.VMEM((size, width), F32),
            pltpu.VMEM((n_blk, 8, size), F32),
            pltpu.VMEM((n_blk, 8, size), F32),
            dma((n_row - 1, chunks)), dma((n_row - 1, chunks)),
            dma((2, d0 - 1)), dma((2, d0 - 1)),
            dma((d0, d1 - 1)), dma((d0, d1 - 1)),
            dma((d0, d1, d2 - 1)), dma((d0, d1, d2 - 1)),
            dma((groups, d2 - 1)), dma((groups, d2 - 1)),
            dma((d0, d1 - 1, 2)), dma((d0, d1 - 1, 2)),
            dma((d0 - 1, 2)), dma((2, d0, 2)),
            dma(dims), dma(dims),
            dma((2,)),
        ],
        compiler_params=pltpu.CompilerParams(
            collective_id=0, has_side_effects=True, vmem_limit_bytes=60 << 20
        ),
        cost_estimate=pl.CostEstimate(
            flops=4 * rows * n_blk * size * width, bytes_accessed=8 << 20,
            transcendentals=rows * n_blk * size,
        ),
    )(coarse, fine, candidates, heat)
    return new, log_norm.reshape(rows)


def solution(mesh):
    return jax.shard_map(
        functools.partial(shards, mesh.shape["blk"], mesh.shape["row"]),
        mesh=mesh,
        in_specs=(P("blk", "row"), P(("blk", "row"), None), P(("blk", "row"), None), P()),
        out_specs=(P(("blk", "row"), None), P(("blk", "row"))),
        check_vma=False,
    )
```

```python
import functools
import math

import jax
import jax.numpy as jnp
from jax import lax
from jax.experimental import pallas as pl
from jax.experimental.pallas import tpu as pltpu
from jax.sharding import PartitionSpec as P

MESH = pl.DeviceIdType.MESH
F32 = jnp.float32
BF16 = jnp.bfloat16
LANES = 256
DEPTH = 3
SPAN = 4


def kernel(
    dims, n_row, x_ref, fine_ref, named_ref, heat_ref, out_ref, lse_ref,
    xbuf, panels, logits, norms, bias, top, peaks, total, weights, part, in_c, send_b, in_b,
    send_a, in_a, send_w, in_w, edge, acc, mass_out, mass_in,
    x_send, x_recv, z_send, z_recv, w_send, w_recv, s_send, s_recv, gx_send, gx_recv, gc_send, gc_recv, c_send, c_recv,
    b_send, b_recv, a_send, a_recv, m_send, m_recv, own_sem,
):
    d0, d1, d2 = dims
    n_blk = d0 * d1 * d2
    row = lax.axis_index("row")
    blk = lax.axis_index("blk")
    i2 = lax.rem(blk, d2)
    i1 = lax.rem(lax.div(blk, d2), d1)
    i0 = lax.div(blk, d1 * d2)
    size = fine_ref.shape[0]
    width = fine_ref.shape[1]
    rows = xbuf.shape[1]
    feats = xbuf.shape[2]
    pair = d2 * size
    half = size // 2
    chunks = x_send.shape[1]
    step = rows // chunks
    blocks, names = named_ref.shape

    def near(i, o, d):
        return lax.rem(i + o + d, d)

    def index(a, b, c):
        return (a * d1 + b) * d2 + c

    def panel(owner):
        return panels.at[pl.ds(pl.multiple_of(owner * size, size), size), :]

    def remote(src, dst, send, recv, to, axis="blk"):
        return pltpu.make_async_remote_copy(
            src_ref=src, dst_ref=dst, send_sem=send, recv_sem=recv,
            device_id={axis: to}, device_id_type=MESH,
        )

    barrier = pltpu.get_barrier_semaphore()
    for d in range(1, n_row):
        pl.semaphore_signal(
            barrier, inc=1, device_id={"row": near(row, d, n_row)}, device_id_type=MESH
        )
    for d in range(1, n_blk):
        pl.semaphore_signal(
            barrier, inc=1, device_id={"blk": near(blk, d, n_blk)}, device_id_type=MESH
        )
    own_x = pltpu.make_async_copy(
        x_ref.at[pl.ds(pl.multiple_of(row * rows, rows), rows), :], xbuf.at[row], own_sem.at[0]
    )
    own_x.start()
    own_panel = pltpu.make_async_copy(fine_ref, panel(blk), own_sem.at[1])
    own_panel.start()
    pl.semaphore_wait(barrier, n_row - 1 + n_blk - 1)

    cut = size - size // 8
    pieces = (pl.ds(0, half), pl.ds(half, cut - half), pl.ds(cut, size - cut))

    def z_copy(way, k, h, own=False):
        sign = 1 - 2 * way
        spot = pl.ds(h * half, half)
        there = panel(index(i0 - sign * (k - 1), i1, i2)).at[spot, :]
        return remote(
            fine_ref.at[spot, :] if own else there, there,
            z_send.at[way, k - 1, h], z_recv.at[way, k - 1, h], index(i0 + sign, i1, i2),
        )

    def w_copy(way, k, o1):
        sign = 1 - 2 * way
        there = panel(index(i0 - sign * (k - 1), near(i1, -o1, d1), i2)).at[pieces[2], :]
        return remote(
            there, there, w_send.at[way, k - 1, o1 - 1], w_recv.at[way, k - 1, o1 - 1],
            index(i0 + sign, i1, i2),
        )

    def x_copy(a, o1, p, own=False):
        there = panel(index(a, i1, i2)).at[pieces[p], :]
        return remote(
            fine_ref.at[pieces[p], :] if own else there, there,
            gx_send.at[a, o1 - 1, p], gx_recv.at[a, o1 - 1, p],
            index(i0, near(i1, o1, d1), i2),
        )

    def c_copy(a, o1, o2, own=False):
        owner = index(a, near(i1, -o1, d1), i2)
        return remote(
            fine_ref if own else panel(owner), panel(owner),
            gc_send.at[a, o1, o2 - 1], gc_recv.at[a, o1, o2 - 1],
            index(i0, i1, near(i2, o2, d2)),
        )

    def inside(i):
        return (i >= 0) & (i < d0)

    for p in (2, 0, 1):
        for o1 in range(1, d1):
            x_copy(i0, o1, p, True).start()
    for way in range(2):
        @pl.when(inside(i0 + 1 - 2 * way))
        def _():
            for h in range(2):
                z_copy(way, 1, h, True).start()
    for o2 in range(1, d2):
        c_copy(i0, 0, o2, True).start()
    points = []
    for c in range(chunks):
        for d in range(1, n_row):
            to = near(row, d, n_row)
            points.append(remote(
                x_ref.at[pl.ds(pl.multiple_of(to * rows + c * step, step), step), :],
                xbuf.at[row, pl.ds(c * step, step), :],
                x_send.at[d - 1, c], x_recv.at[d - 1, c], to, "row",
            ))

    def send_points(c):
        for copy in points[c * (n_row - 1):(c + 1) * (n_row - 1)]:
            copy.start()

    for c in range(chunks):
        send_points(c)
    for o1 in range(1, d1):
        x_copy(i0, o1, 2).wait_recv()
    for way in range(2):
        @pl.when(inside(i0 + 1 - 2 * way))
        def _():
            for o1 in range(1, d1):
                w_copy(way, 1, o1).start()

    @pl.loop(0, n_blk)
    def _(g):
        for b in range(blocks):
            hit = named_ref[b, 0] == g
            for j in range(1, names):
                hit = hit | (named_ref[b, j] == g)
            bias[g, :, b * (rows // blocks):(b + 1) * (rows // blocks)] = jnp.full(
                (1, rows // blocks), jnp.where(hit, 0.0, -1e30), F32
            )

    scale = 1.0 / (jnp.full((1, LANES), heat_ref[0], F32) * math.sqrt(width))
    top[...] = jnp.full(top.shape, -1e30, F32)
    total[...] = jnp.zeros(total.shape, F32)

    def measure(a, o1):
        for o2 in range(1, d2):
            c_copy(a, o1, o2).wait_recv()
        base = pl.multiple_of(index(a, near(i1, -o1, d1), 0) * size, pair)
        whole = panels[pl.ds(base, pair), :].astype(F32)
        norms[pl.ds(base, pair), :] = jnp.broadcast_to(
            jnp.sum(whole * whole, axis=1, keepdims=True), (pair, 128)
        ) * scale[:, :128]
        return base

    def score(a, o1):
        base = measure(a, o1)
        left = panels[pl.ds(base, pair), pl.ds(pl.multiple_of(row * feats, feats), feats)]

        @pl.loop(0, rows // LANES)
        def _(c):
            lane = pl.multiple_of(c * LANES, LANES)
            logits[pl.ds(base, pair), pl.ds(lane, LANES)] = lax.dot_general(
                left, xbuf[row, pl.ds(lane, LANES), :], (((1,), (1,)), ((), ())),
                preferred_element_type=F32,
            )

    def z_event(way, k, h):
        sign = 1 - 2 * way
        a = i0 - sign * k

        @pl.when(inside(a))
        def _():
            z_copy(way, k, h).wait_recv()
            if k < d0 - 1:
                @pl.when(inside(i0 + sign))
                def _():
                    z_copy(way, k + 1, h).start()
            for o1 in range(1, d1):
                x_copy(a, o1, h).start()
            if h == 1:
                for o2 in range(1, d2):
                    c_copy(a, 0, o2).start()

    def w_event(way, k):
        sign = 1 - 2 * way

        @pl.when(inside(i0 - sign * k))
        def _():
            for o1 in range(1, d1):
                w_copy(way, k, o1).wait_recv()
            if k < d0 - 1:
                @pl.when(inside(i0 + sign))
                def _():
                    for o1 in range(1, d1):
                        w_copy(way, k + 1, o1).start()

    def x_arrival(a):
        for o1 in range(1, d1):
            for p in range(2):
                x_copy(a, o1, p).wait_recv()
            for o2 in range(1, d2):
                c_copy(a, o1, o2).start()

    def x_event(a):
        x_arrival(a)
        for o1 in range(d1):
            score(a, o1)

    joint = max(1, min(d1, SPAN // d2))

    def fuse(g, c, count, full=False):
        lanes = pl.ds(c * LANES, LANES)
        base = pl.multiple_of(g * pair, pair)
        tile = pl.ds(base, count * pair)
        dots = None if full else logits[tile, lanes]
        for d in range(0 if full else 1, n_row):
            other = near(row, d, n_row)
            term = lax.dot_general(
                panels[tile, pl.ds(pl.multiple_of(other * feats, feats), feats)],
                xbuf[other, lanes, :], (((1,), (1,)), ((), ())),
                preferred_element_type=F32,
            )
            dots = term if dots is None else dots + term
        values = []
        old = top[0:1, lanes]
        best = jnp.broadcast_to(old, (8, LANES))
        for j in range(count * d2):
            norm = norms[pl.ds(base + j * size, size), :1]
            value = dots[j * size:(j + 1) * size] * (2.0 * scale) - norm
            values.append(value + bias[g * d2 + j, :, lanes])
            best = jnp.maximum(best, jnp.max(values[j].reshape(size // 8, 8, LANES), axis=0))
        best = jnp.max(best, axis=0, keepdims=True)
        added = total[:, lanes] * jnp.exp(old - best)
        for j in range(count * d2):
            value = jnp.exp(values[j] - best)
            logits[pl.ds(base + j * size, size), lanes] = value
            added = added + jnp.sum(value.reshape(size // 8, 8, LANES), axis=0)
        total[:, lanes] = added
        top[:, lanes] = jnp.broadcast_to(best, (8, LANES))
        for j in range(count):
            peaks[g + j, :, lanes] = best

    own_x.wait()
    own_panel.wait()
    late = jnp.where(i0 < d0 // 2, d0 - 1, 0)
    for k in range(1, d0):
        for h in range(2):
            for way in range(2):
                z_event(way, k, h)
        for way in range(2):
            w_event(way, k)
        if k == 1:
            x_event(i0)
        else:
            for way in range(2):
                a = i0 - (1 - 2 * way) * (k - 1)

                @pl.when(inside(a) & (a != late))
                def _():
                    x_event(a)
    score(late, 0)

    each = d1 // joint
    first = jnp.where(late == 0, d1, 0)
    for c in range(chunks):
        if c == chunks - 1:
            x_arrival(late)
        for copy in points[c * (n_row - 1):(c + 1) * (n_row - 1)]:
            copy.wait_recv()
        fuse(late * d1 + i1, c, 1)

        @pl.loop(0, (d0 - 1) * each)
        def _(g):
            fuse(first + g * joint, c, joint)

    for o1 in range(1, d1):
        measure(late, o1)
        g = late * d1 + near(i1, -o1, d1)
        for c in range(chunks):
            fuse(g, c, 1, True)

    summed = jnp.sum(total[...], axis=0, keepdims=True)
    lse_ref[...] = top[0:1, :] + jnp.log(summed)
    total[...] = jnp.broadcast_to(1.0 / summed, total.shape)

    def target(k):
        value = 0
        for z in range(d0):
            far = sorted(range(d0), key=lambda t: (-abs(t - z), t if z >= d0 // 2 else -t))
            value = jnp.where(i0 == z, far[k], value)
        return value

    targets = [target(k) for k in range(d0)]

    def c_sum(k, o1, o2):
        j = near(i2, o2, d2)
        return remote(
            part.at[k * d1 + o1, pl.ds(pl.multiple_of(j * size, size), size), :],
            in_c.at[k * d1 + o1, o2 - 1], c_send.at[k * d1 + o1, o2 - 1],
            c_recv.at[k * d1 + o1, o2 - 1], index(i0, i1, j),
        )

    def b_sum(k, o1, h):
        spot = pl.ds(h * half, half if h == 0 or k == d0 - 1 else cut - half)
        return remote(
            send_b.at[k, o1 - 1, spot, :], in_b.at[k, o1 - 1, spot, :],
            b_send.at[k, o1 - 1, h], b_recv.at[k, o1 - 1, h],
            index(i0, near(i1, o1, d1), i2),
        )

    def a_sum(k, h, way, goal):
        spot = pl.ds(h * half, half)
        return remote(
            send_a.at[min(k, d0 - 2), spot, :], in_a.at[way, goal, spot, :],
            a_send.at[min(k, d0 - 2), h], a_recv.at[way, goal, h],
            index(near(i0, 1 - 2 * way, d0), i1, i2),
        )

    def w_sum(k, o1, way, goal):
        return remote(
            send_w.at[min(k, d0 - 2), o1 - 1], in_w.at[way, goal, o1 - 1],
            s_send.at[min(k, d0 - 2), o1 - 1], s_recv.at[way, goal, o1 - 1],
            index(near(i0, 1 - 2 * way, d0), i1, i2),
        )

    def around(k):
        goal = targets[k]
        last = k == d0 - 1
        for o1 in range(1, d1):
            edge[...] = send_b[k, o1 - 1, cut:, :].astype(F32)
            for way in (0, 1) if last else (jnp.where(goal > i0, 0, 1),):
                @pl.when(inside(i0 - 1 + 2 * way))
                def _():
                    w_sum(k, o1, way, goal).wait_recv()
                    edge[...] += in_w[way, goal, o1 - 1].astype(F32)

            if last:
                send_b[k, o1 - 1, cut:, :] = edge[...].astype(BF16)
            else:
                send_w[k, o1 - 1] = edge[...].astype(BF16)
                w_sum(k, o1, way, goal).start()

    def m_sum(o0, o1, o2):
        to = index(near(i0, o0, d0), near(i1, o1, d1), near(i2, o2, d2))
        return remote(
            mass_out.at[to], mass_in.at[blk], m_send.at[o0, o1, o2], m_recv.at[o0, o1, o2], to
        )

    def weigh(k, o1):
        owner = index(targets[k], near(i1, o1, d1), 0)
        base = pl.multiple_of(owner * size, pair)
        factor = jnp.exp(peaks[lax.div(owner, d2)] - top[0:1, :]) * total[0:1, :]
        weights[...] = (logits[pl.ds(base, pair), :] * factor).astype(BF16)

        @pl.loop(0, n_row)
        def _(s):
            part[k * d1 + o1, :, pl.ds(pl.multiple_of(s * feats, feats), feats)] = jnp.dot(
                weights[...], xbuf[s], preferred_element_type=F32
            ).astype(BF16)

        for o2 in range(1, d2):
            c_sum(k, o1, o2).start()
        mass = lax.dot_general(
            jnp.ones((8, rows), BF16), weights[...], (((1,), (1,)), ((), ())),
            preferred_element_type=F32,
        )
        for j in range(d2):
            mass_out[owner + j] = mass[:, j * size:(j + 1) * size]

    def chip_sum(k, o1, begin, count):
        start = pl.multiple_of(i2 * size + begin, half)
        value = part[k * d1 + o1, pl.ds(start, count), :].astype(F32)
        for o2 in range(1, d2):
            value = value + in_c[k * d1 + o1, o2 - 1, begin:begin + count, :].astype(F32)
        return value

    def ready(k):
        for o1 in range(1, d1):
            for o2 in range(1, d2):
                c_sum(k, o1, o2).wait_recv()
            send_b[k, o1 - 1] = chip_sum(k, o1, 0, size).astype(BF16)

    halves = [(k, h) for k in range(d0) for h in range(2)]

    def pass_on(position):
        if position < len(halves):
            k, h = halves[position]
            for o1 in range(1, d1):
                b_sum(k, o1, h).start()

    started = 0
    for k in range(d0):
        for o1 in range(1, d1):
            weigh(k, o1)
        if k > 0:
            ready(k - 1)
            while started < min(DEPTH, 2 * k):
                pass_on(started)
                started += 1
    weigh(0, 0)
    ready(d0 - 1)
    while started < min(DEPTH, 2 * d0):
        pass_on(started)
        started += 1

    for position, (k, h) in enumerate(halves):
        if h == 0 and k < d0 - 1:
            weigh(k + 1, 0)
            if k == d0 - 2:
                for o0 in range(d0):
                    for o1 in range(d1):
                        for o2 in range(d2):
                            if (o0, o1, o2) != (0, 0, 0):
                                m_sum(o0, o1, o2).start()
        for o1 in range(1, d1):
            b_sum(k, o1, h).wait_recv()
        if position + DEPTH < len(halves) - 1:
            pass_on(position + DEPTH)
        if h == 0 and k < d0 - 1:
            around(k)
        if position + DEPTH == len(halves) - 1:
            around(d0 - 1)
            pass_on(position + DEPTH)
        if h == 0:
            for o2 in range(1, d2):
                c_sum(k, 0, o2).wait_recv()
        value = chip_sum(k, 0, h * half, half)
        for o1 in range(1, d1):
            if h == 0 or k == d0 - 1:
                value = value + in_b[k, o1 - 1, h * half:(h + 1) * half, :].astype(F32)
        spot = pl.ds(h * half, half)
        acc[spot, :] = value
        if h == 1 and k < d0 - 1:
            for o1 in range(1, d1):
                acc[half:cut, :] += in_b[k, o1 - 1, half:cut, :].astype(F32)
        goal = targets[k]
        if k < d0 - 1:
            way = jnp.where(goal > i0, 0, 1)

            @pl.when(inside(i0 - 1 + 2 * way))
            def _():
                a_sum(k, h, way, goal).wait_recv()
                acc[spot, :] += in_a[way, goal, spot, :].astype(F32)

            send_a[k, spot, :] = acc[spot, :].astype(BF16)
            a_sum(k, h, way, goal).start()

    mass_in[blk] = mass_out[blk]
    mass = None
    for o0 in range(d0):
        for o1 in range(d1):
            for o2 in range(d2):
                if (o0, o1, o2) != (0, 0, 0):
                    m_sum(o0, o1, o2).wait_recv()
    mass = mass_in[0]
    for g in range(1, n_blk):
        mass = mass + mass_in[g]
    column = jnp.broadcast_to(mass[0:1, :], (size, size)).T[:, 0:1] + 1.0
    acc[...] += panels[pl.ds(pl.multiple_of(blk * size, size), size), :].astype(F32)
    for h in range(2):
        spot = pl.ds(h * half, half)
        for way in range(2):
            @pl.when(inside(i0 - 1 + 2 * way))
            def _():
                a_sum(d0 - 1, h, way, i0).wait_recv()
                acc[spot, :] += in_a[way, i0, spot, :].astype(F32)
        out_ref[spot, :] = (acc[spot, :] / column[h * half:(h + 1) * half]).astype(BF16)

    for copy in points:
        copy.wait_send()
    for way in range(2):
        sign = 1 - 2 * way
        for k in range(1, d0):
            @pl.when(inside(i0 + sign) & inside(i0 - sign * (k - 1)))
            def _():
                for h in range(2):
                    z_copy(way, k, h).wait_send()
                for o1 in range(1, d1):
                    w_copy(way, k, o1).wait_send()
    for o1 in range(1, d1):
        x_copy(i0, o1, 2).wait_send()
    for a in range(d0):
        for o1 in range(1, d1):
            for p in range(2):
                x_copy(a, o1, p).wait_send()
        for o1 in range(d1):
            for o2 in range(1, d2):
                c_copy(a, o1, o2).wait_send()
                c_sum(a, o1, o2).wait_send()
        for h in range(2):
            for o1 in range(1, d1):
                b_sum(a, o1, h).wait_send()
            if a < d0 - 1:
                a_sum(a, h, 0, i0).wait_send()
        if a < d0 - 1:
            for o1 in range(1, d1):
                w_sum(a, o1, 0, i0).wait_send()
    for o0 in range(d0):
        for o1 in range(d1):
            for o2 in range(d2):
                if (o0, o1, o2) != (0, 0, 0):
                    m_sum(o0, o1, o2).wait_send()


def shards(n_blk, n_row, coarse, fine, candidates, heat):
    inner = 2 if n_blk < 32 else 4
    dims = (n_blk // (inner * inner), inner, inner)
    d0, d1, d2 = dims
    size, width = fine.shape
    rows = coarse.shape[0] // n_row
    feats = coarse.shape[1]
    vmem = pl.BlockSpec(memory_space=pltpu.VMEM)
    hbm = pl.BlockSpec(memory_space=pl.ANY)
    smem = pl.BlockSpec(memory_space=pltpu.SMEM)
    groups = d0 * d1
    chunks = rows // LANES
    dma = pltpu.SemaphoreType.DMA
    new, log_norm = pl.pallas_call(
        functools.partial(kernel, dims, n_row),
        out_shape=(
            jax.ShapeDtypeStruct((size, width), BF16),
            jax.ShapeDtypeStruct((1, rows), F32),
        ),
        in_specs=[hbm, hbm, smem, smem],
        out_specs=(vmem, vmem),
        scratch_shapes=[
            pltpu.VMEM((n_row, rows, feats), BF16),
            pltpu.VMEM((n_blk * size, width), BF16),
            pltpu.VMEM((n_blk * size, rows), F32),
            pltpu.VMEM((n_blk * size, 128), F32),
            pltpu.VMEM((n_blk, 1, rows), F32),
            pltpu.VMEM((8, rows), F32),
            pltpu.VMEM((groups, 1, rows), F32),
            pltpu.VMEM((8, rows), F32),
            pltpu.VMEM((d2 * size, rows), BF16),
            pltpu.VMEM((groups, d2 * size, width), BF16),
            pltpu.VMEM((groups, d2 - 1, size, width), BF16),
            pltpu.VMEM((d0, d1 - 1, size, width), BF16),
            pltpu.VMEM((d0, d1 - 1, size, width), BF16),
            pltpu.VMEM((d0 - 1, size, width), BF16),
            pltpu.VMEM((2, d0, size, width), BF16),
            pltpu.VMEM((d0 - 1, d1 - 1, size // 8, width), BF16),
            pltpu.VMEM((2, d0, d1 - 1, size // 8, width), BF16),
            pltpu.VMEM((size // 8, width), F32),
            pltpu.VMEM((size, width), F32),
            pltpu.VMEM((n_blk, 8, size), F32),
            pltpu.VMEM((n_blk, 8, size), F32),
            dma((n_row - 1, chunks)), dma((n_row - 1, chunks)),
            dma((2, d0 - 1, 2)), dma((2, d0 - 1, 2)),
            dma((2, d0 - 1, d1 - 1)), dma((2, d0 - 1, d1 - 1)),
            dma((d0 - 1, d1 - 1)), dma((2, d0, d1 - 1)),
            dma((d0, d1 - 1, 3)), dma((d0, d1 - 1, 3)),
            dma((d0, d1, d2 - 1)), dma((d0, d1, d2 - 1)),
            dma((groups, d2 - 1)), dma((groups, d2 - 1)),
            dma((d0, d1 - 1, 2)), dma((d0, d1 - 1, 2)),
            dma((d0 - 1, 2)), dma((2, d0, 2)),
            dma(dims), dma(dims),
            dma((2,)),
        ],
        compiler_params=pltpu.CompilerParams(
            collective_id=0, has_side_effects=True, vmem_limit_bytes=60 << 20
        ),
        cost_estimate=pl.CostEstimate(
            flops=4 * rows * n_blk * size * width, bytes_accessed=8 << 20,
            transcendentals=rows * n_blk * size,
        ),
    )(coarse, fine, candidates, heat)
    return new, log_norm.reshape(rows)


def solution(mesh):
    return jax.shard_map(
        functools.partial(shards, mesh.shape["blk"], mesh.shape["row"]),
        mesh=mesh,
        in_specs=(P("blk", "row"), P(("blk", "row"), None), P(("blk", "row"), None), P()),
        out_specs=(P(("blk", "row"), None), P(("blk", "row"))),
        check_vma=False,
    )
```

```python
import functools
import math

import jax
import jax.numpy as jnp
from jax import lax
from jax.experimental import pallas as pl
from jax.experimental.pallas import tpu as pltpu
from jax.sharding import PartitionSpec as P

MESH = pl.DeviceIdType.MESH
F32 = jnp.float32
BF16 = jnp.bfloat16
LANES = 256
DEPTH = 4
SPAN = 4


def kernel(
    dims, n_row, x_ref, fine_ref, named_ref, heat_ref, out_ref, lse_ref,
    xbuf, panels, logits, norms, bias, top, peaks, total, weights, part, in_c, send_b, in_b,
    send_a, in_a, acc, mass_out, mass_in,
    x_send, x_recv, z_send, z_recv, gx_send, gx_recv, gc_send, gc_recv, c_send, c_recv,
    b_send, b_recv, a_send, a_recv, m_send, m_recv, own_sem,
):
    d0, d1, d2 = dims
    n_blk = d0 * d1 * d2
    row = lax.axis_index("row")
    blk = lax.axis_index("blk")
    i2 = lax.rem(blk, d2)
    i1 = lax.rem(lax.div(blk, d2), d1)
    i0 = lax.div(blk, d1 * d2)
    size = fine_ref.shape[0]
    width = fine_ref.shape[1]
    rows = xbuf.shape[1]
    feats = xbuf.shape[2]
    pair = d2 * size
    half = size // 2
    chunks = x_send.shape[1]
    step = rows // chunks
    blocks, names = named_ref.shape

    def near(i, o, d):
        return lax.rem(i + o + d, d)

    def index(a, b, c):
        return (a * d1 + b) * d2 + c

    def panel(owner):
        return panels.at[pl.ds(pl.multiple_of(owner * size, size), size), :]

    def remote(src, dst, send, recv, to, axis="blk"):
        return pltpu.make_async_remote_copy(
            src_ref=src, dst_ref=dst, send_sem=send, recv_sem=recv,
            device_id={axis: to}, device_id_type=MESH,
        )

    barrier = pltpu.get_barrier_semaphore()
    for d in range(1, n_row):
        pl.semaphore_signal(
            barrier, inc=1, device_id={"row": near(row, d, n_row)}, device_id_type=MESH
        )
    for d in range(1, n_blk):
        pl.semaphore_signal(
            barrier, inc=1, device_id={"blk": near(blk, d, n_blk)}, device_id_type=MESH
        )
    own_x = pltpu.make_async_copy(
        x_ref.at[pl.ds(pl.multiple_of(row * rows, rows), rows), :], xbuf.at[row], own_sem.at[0]
    )
    own_x.start()
    own_panel = pltpu.make_async_copy(fine_ref, panel(blk), own_sem.at[1])
    own_panel.start()
    pl.semaphore_wait(barrier, n_row - 1 + n_blk - 1)

    def z_copy(way, k, own=False):
        sign = 1 - 2 * way
        owner = index(i0 - sign * (k - 1), i1, i2)
        return remote(
            fine_ref if own else panel(owner), panel(owner),
            z_send.at[way, k - 1], z_recv.at[way, k - 1], index(i0 + sign, i1, i2),
        )

    def x_copy(a, o1, own=False):
        owner = index(a, i1, i2)
        return remote(
            fine_ref if own else panel(owner), panel(owner),
            gx_send.at[a, o1 - 1], gx_recv.at[a, o1 - 1], index(i0, near(i1, o1, d1), i2),
        )

    def c_copy(a, o1, o2, own=False):
        owner = index(a, near(i1, -o1, d1), i2)
        return remote(
            fine_ref if own else panel(owner), panel(owner),
            gc_send.at[a, o1, o2 - 1], gc_recv.at[a, o1, o2 - 1],
            index(i0, i1, near(i2, o2, d2)),
        )

    def inside(i):
        return (i >= 0) & (i < d0)

    for o1 in range(1, d1):
        x_copy(i0, o1, True).start()
    for way in range(2):
        @pl.when(inside(i0 + 1 - 2 * way))
        def _():
            z_copy(way, 1, True).start()
    for o2 in range(1, d2):
        c_copy(i0, 0, o2, True).start()
    points = []
    for c in range(chunks):
        for d in range(1, n_row):
            to = near(row, d, n_row)
            points.append(remote(
                x_ref.at[pl.ds(pl.multiple_of(to * rows + c * step, step), step), :],
                xbuf.at[row, pl.ds(c * step, step), :],
                x_send.at[d - 1, c], x_recv.at[d - 1, c], to, "row",
            ))

    def send_points(c):
        for copy in points[c * (n_row - 1):(c + 1) * (n_row - 1)]:
            copy.start()

    for c in range(chunks):
        send_points(c)

    @pl.loop(0, n_blk)
    def _(g):
        for b in range(blocks):
            hit = named_ref[b, 0] == g
            for j in range(1, names):
                hit = hit | (named_ref[b, j] == g)
            bias[g, :, b * (rows // blocks):(b + 1) * (rows // blocks)] = jnp.full(
                (1, rows // blocks), jnp.where(hit, 0.0, -1e30), F32
            )

    scale = 1.0 / (jnp.full((1, LANES), heat_ref[0], F32) * math.sqrt(width))
    top[...] = jnp.full(top.shape, -1e30, F32)
    total[...] = jnp.zeros(total.shape, F32)

    def measure(a, o1):
        for o2 in range(1, d2):
            c_copy(a, o1, o2).wait_recv()
        base = pl.multiple_of(index(a, near(i1, -o1, d1), 0) * size, pair)
        whole = panels[pl.ds(base, pair), :].astype(F32)
        norms[pl.ds(base, pair), :] = jnp.broadcast_to(
            jnp.sum(whole * whole, axis=1, keepdims=True), (pair, 128)
        ) * scale[:, :128]
        return base

    def score(a, o1):
        base = measure(a, o1)
        left = panels[pl.ds(base, pair), pl.ds(pl.multiple_of(row * feats, feats), feats)]

        @pl.loop(0, rows // LANES)
        def _(c):
            lane = pl.multiple_of(c * LANES, LANES)
            logits[pl.ds(base, pair), pl.ds(lane, LANES)] = lax.dot_general(
                left, xbuf[row, pl.ds(lane, LANES), :], (((1,), (1,)), ((), ())),
                preferred_element_type=F32,
            )

    def z_event(way, k):
        sign = 1 - 2 * way

        @pl.when(inside(i0 - sign * k))
        def _():
            z_copy(way, k).wait_recv()
            if k < d0 - 1:
                @pl.when(inside(i0 + sign))
                def _():
                    z_copy(way, k + 1).start()
            a = i0 - sign * k
            for o1 in range(1, d1):
                x_copy(a, o1).start()
            for o2 in range(1, d2):
                c_copy(a, 0, o2).start()

    def x_arrival(a):
        for o1 in range(1, d1):
            x_copy(a, o1).wait_recv()
            for o2 in range(1, d2):
                c_copy(a, o1, o2).start()

    def x_event(a):
        x_arrival(a)
        for o1 in range(d1):
            score(a, o1)

    joint = max(1, min(d1, SPAN // d2))

    def fuse(g, c, count, full=False):
        lanes = pl.ds(c * LANES, LANES)
        base = pl.multiple_of(g * pair, pair)
        tile = pl.ds(base, count * pair)
        dots = None if full else logits[tile, lanes]
        for d in range(0 if full else 1, n_row):
            other = near(row, d, n_row)
            term = lax.dot_general(
                panels[tile, pl.ds(pl.multiple_of(other * feats, feats), feats)],
                xbuf[other, lanes, :], (((1,), (1,)), ((), ())),
                preferred_element_type=F32,
            )
            dots = term if dots is None else dots + term
        values = []
        old = top[0:1, lanes]
        best = jnp.broadcast_to(old, (8, LANES))
        for j in range(count * d2):
            norm = norms[pl.ds(base + j * size, size), :1]
            value = dots[j * size:(j + 1) * size] * (2.0 * scale) - norm
            values.append(value + bias[g * d2 + j, :, lanes])
            best = jnp.maximum(best, jnp.max(values[j].reshape(size // 8, 8, LANES), axis=0))
        best = jnp.max(best, axis=0, keepdims=True)
        added = total[:, lanes] * jnp.exp(old - best)
        for j in range(count * d2):
            value = jnp.exp(values[j] - best)
            logits[pl.ds(base + j * size, size), lanes] = value
            added = added + jnp.sum(value.reshape(size // 8, 8, LANES), axis=0)
        total[:, lanes] = added
        top[:, lanes] = jnp.broadcast_to(best, (8, LANES))
        for j in range(count):
            peaks[g + j, :, lanes] = best

    own_x.wait()
    own_panel.wait()
    late = jnp.where(i0 < d0 // 2, d0 - 1, 0)
    for k in range(1, d0):
        for way in range(2):
            z_event(way, k)
        if k == 1:
            x_event(i0)
        else:
            for way in range(2):
                a = i0 - (1 - 2 * way) * (k - 1)

                @pl.when(inside(a) & (a != late))
                def _():
                    x_event(a)
    score(late, 0)

    each = d1 // joint
    first = jnp.where(late == 0, d1, 0)
    for c in range(chunks):
        if c == chunks - 1:
            x_arrival(late)
        for copy in points[c * (n_row - 1):(c + 1) * (n_row - 1)]:
            copy.wait_recv()
        fuse(late * d1 + i1, c, 1)

        @pl.loop(0, (d0 - 1) * each)
        def _(g):
            fuse(first + g * joint, c, joint)

    for o1 in range(1, d1):
        measure(late, o1)
        g = late * d1 + near(i1, -o1, d1)
        for c in range(chunks):
            fuse(g, c, 1, True)

    summed = jnp.sum(total[...], axis=0, keepdims=True)
    lse_ref[...] = top[0:1, :] + jnp.log(summed)
    total[...] = jnp.broadcast_to(1.0 / summed, total.shape)

    def target(k):
        value = 0
        for z in range(d0):
            far = sorted(range(d0), key=lambda t: (-abs(t - z), t if z >= d0 // 2 else -t))
            value = jnp.where(i0 == z, far[k], value)
        return value

    targets = [target(k) for k in range(d0)]

    def c_sum(k, o1, o2):
        j = near(i2, o2, d2)
        return remote(
            part.at[k * d1 + o1, pl.ds(pl.multiple_of(j * size, size), size), :],
            in_c.at[k * d1 + o1, o2 - 1], c_send.at[k * d1 + o1, o2 - 1],
            c_recv.at[k * d1 + o1, o2 - 1], index(i0, i1, j),
        )

    def b_sum(k, o1, h):
        spot = pl.ds(h * half, half)
        return remote(
            send_b.at[k, o1 - 1, spot, :], in_b.at[k, o1 - 1, spot, :],
            b_send.at[k, o1 - 1, h], b_recv.at[k, o1 - 1, h],
            index(i0, near(i1, o1, d1), i2),
        )

    def a_sum(k, h, way, goal):
        spot = pl.ds(h * half, half)
        return remote(
            send_a.at[min(k, d0 - 2), spot, :], in_a.at[way, goal, spot, :],
            a_send.at[min(k, d0 - 2), h], a_recv.at[way, goal, h],
            index(near(i0, 1 - 2 * way, d0), i1, i2),
        )

    def m_sum(o0, o1, o2):
        to = index(near(i0, o0, d0), near(i1, o1, d1), near(i2, o2, d2))
        return remote(
            mass_out.at[to], mass_in.at[blk], m_send.at[o0, o1, o2], m_recv.at[o0, o1, o2], to
        )

    def weigh(k, o1):
        owner = index(targets[k], near(i1, o1, d1), 0)
        base = pl.multiple_of(owner * size, pair)
        factor = jnp.exp(peaks[lax.div(owner, d2)] - top[0:1, :]) * total[0:1, :]
        weights[...] = (logits[pl.ds(base, pair), :] * factor).astype(BF16)

        @pl.loop(0, n_row)
        def _(s):
            part[k * d1 + o1, :, pl.ds(pl.multiple_of(s * feats, feats), feats)] = jnp.dot(
                weights[...], xbuf[s], preferred_element_type=F32
            ).astype(BF16)

        for o2 in range(1, d2):
            c_sum(k, o1, o2).start()
        mass = lax.dot_general(
            jnp.ones((8, rows), BF16), weights[...], (((1,), (1,)), ((), ())),
            preferred_element_type=F32,
        )
        for j in range(d2):
            mass_out[owner + j] = mass[:, j * size:(j + 1) * size]

    def chip_sum(k, o1, begin, count):
        start = pl.multiple_of(i2 * size + begin, half)
        value = part[k * d1 + o1, pl.ds(start, count), :].astype(F32)
        for o2 in range(1, d2):
            value = value + in_c[k * d1 + o1, o2 - 1, begin:begin + count, :].astype(F32)
        return value

    def ready(k):
        for o1 in range(1, d1):
            for o2 in range(1, d2):
                c_sum(k, o1, o2).wait_recv()
            send_b[k, o1 - 1] = chip_sum(k, o1, 0, size).astype(BF16)

    halves = [(k, h) for k in range(d0) for h in range(2)]

    def pass_on(position):
        if position < len(halves):
            k, h = halves[position]
            for o1 in range(1, d1):
                b_sum(k, o1, h).start()

    started = 0
    for k in range(d0):
        for o1 in range(1, d1):
            weigh(k, o1)
        done = max(k, 1)
        if k != 1:
            ready(done - 1)
        while started < min(DEPTH, 2 * done):
            pass_on(started)
            started += 1
    weigh(0, 0)
    ready(d0 - 1)
    while started < min(DEPTH, 2 * d0):
        pass_on(started)
        started += 1

    for position, (k, h) in enumerate(halves):
        for o1 in range(1, d1):
            b_sum(k, o1, h).wait_recv()
        pass_on(position + DEPTH)
        if h == 0:
            for o2 in range(1, d2):
                c_sum(k, 0, o2).wait_recv()
        value = chip_sum(k, 0, h * half, half)
        for o1 in range(1, d1):
            value = value + in_b[k, o1 - 1, h * half:(h + 1) * half, :].astype(F32)
        spot = pl.ds(h * half, half)
        acc[spot, :] = value
        goal = targets[k]
        if k < d0 - 1:
            way = jnp.where(goal > i0, 0, 1)

            @pl.when(inside(i0 - 1 + 2 * way))
            def _():
                a_sum(k, h, way, goal).wait_recv()
                acc[spot, :] += in_a[way, goal, spot, :].astype(F32)

            send_a[k, spot, :] = acc[spot, :].astype(BF16)
            a_sum(k, h, way, goal).start()
            if h == 0:
                weigh(k + 1, 0)
                if k == d0 - 2:
                    for o0 in range(d0):
                        for o1 in range(d1):
                            for o2 in range(d2):
                                if (o0, o1, o2) != (0, 0, 0):
                                    m_sum(o0, o1, o2).start()

    mass_in[blk] = mass_out[blk]
    mass = None
    for o0 in range(d0):
        for o1 in range(d1):
            for o2 in range(d2):
                if (o0, o1, o2) != (0, 0, 0):
                    m_sum(o0, o1, o2).wait_recv()
    mass = mass_in[0]
    for g in range(1, n_blk):
        mass = mass + mass_in[g]
    column = jnp.broadcast_to(mass[0:1, :], (size, size)).T[:, 0:1] + 1.0
    acc[...] += panels[pl.ds(pl.multiple_of(blk * size, size), size), :].astype(F32)
    for h in range(2):
        spot = pl.ds(h * half, half)
        for way in range(2):
            @pl.when(inside(i0 - 1 + 2 * way))
            def _():
                a_sum(d0 - 1, h, way, i0).wait_recv()
                acc[spot, :] += in_a[way, i0, spot, :].astype(F32)
        out_ref[spot, :] = (acc[spot, :] / column[h * half:(h + 1) * half]).astype(BF16)

    for copy in points:
        copy.wait_send()
    for way in range(2):
        sign = 1 - 2 * way
        for k in range(1, d0):
            @pl.when(inside(i0 + sign) & inside(i0 - sign * (k - 1)))
            def _():
                z_copy(way, k).wait_send()
    for a in range(d0):
        for o1 in range(1, d1):
            x_copy(a, o1).wait_send()
        for o1 in range(d1):
            for o2 in range(1, d2):
                c_copy(a, o1, o2).wait_send()
                c_sum(a, o1, o2).wait_send()
        for h in range(2):
            for o1 in range(1, d1):
                b_sum(a, o1, h).wait_send()
            if a < d0 - 1:
                a_sum(a, h, 0, i0).wait_send()
    for o0 in range(d0):
        for o1 in range(d1):
            for o2 in range(d2):
                if (o0, o1, o2) != (0, 0, 0):
                    m_sum(o0, o1, o2).wait_send()


def shards(n_blk, n_row, coarse, fine, candidates, heat):
    inner = 2 if n_blk < 32 else 4
    dims = (n_blk // (inner * inner), inner, inner)
    d0, d1, d2 = dims
    size, width = fine.shape
    rows = coarse.shape[0] // n_row
    feats = coarse.shape[1]
    vmem = pl.BlockSpec(memory_space=pltpu.VMEM)
    hbm = pl.BlockSpec(memory_space=pl.ANY)
    smem = pl.BlockSpec(memory_space=pltpu.SMEM)
    groups = d0 * d1
    chunks = rows // LANES
    dma = pltpu.SemaphoreType.DMA
    new, log_norm = pl.pallas_call(
        functools.partial(kernel, dims, n_row),
        out_shape=(
            jax.ShapeDtypeStruct((size, width), BF16),
            jax.ShapeDtypeStruct((1, rows), F32),
        ),
        in_specs=[hbm, hbm, smem, smem],
        out_specs=(vmem, vmem),
        scratch_shapes=[
            pltpu.VMEM((n_row, rows, feats), BF16),
            pltpu.VMEM((n_blk * size, width), BF16),
            pltpu.VMEM((n_blk * size, rows), F32),
            pltpu.VMEM((n_blk * size, 128), F32),
            pltpu.VMEM((n_blk, 1, rows), F32),
            pltpu.VMEM((8, rows), F32),
            pltpu.VMEM((groups, 1, rows), F32),
            pltpu.VMEM((8, rows), F32),
            pltpu.VMEM((d2 * size, rows), BF16),
            pltpu.VMEM((groups, d2 * size, width), BF16),
            pltpu.VMEM((groups, d2 - 1, size, width), BF16),
            pltpu.VMEM((d0, d1 - 1, size, width), BF16),
            pltpu.VMEM((d0, d1 - 1, size, width), BF16),
            pltpu.VMEM((d0 - 1, size, width), BF16),
            pltpu.VMEM((2, d0, size, width), BF16),
            pltpu.VMEM((size, width), F32),
            pltpu.VMEM((n_blk, 8, size), F32),
            pltpu.VMEM((n_blk, 8, size), F32),
            dma((n_row - 1, chunks)), dma((n_row - 1, chunks)),
            dma((2, d0 - 1)), dma((2, d0 - 1)),
            dma((d0, d1 - 1)), dma((d0, d1 - 1)),
            dma((d0, d1, d2 - 1)), dma((d0, d1, d2 - 1)),
            dma((groups, d2 - 1)), dma((groups, d2 - 1)),
            dma((d0, d1 - 1, 2)), dma((d0, d1 - 1, 2)),
            dma((d0 - 1, 2)), dma((2, d0, 2)),
            dma(dims), dma(dims),
            dma((2,)),
        ],
        compiler_params=pltpu.CompilerParams(
            collective_id=0, has_side_effects=True, vmem_limit_bytes=60 << 20
        ),
        cost_estimate=pl.CostEstimate(
            flops=4 * rows * n_blk * size * width, bytes_accessed=8 << 20,
            transcendentals=rows * n_blk * size,
        ),
    )(coarse, fine, candidates, heat)
    return new, log_norm.reshape(rows)


def solution(mesh):
    return jax.shard_map(
        functools.partial(shards, mesh.shape["blk"], mesh.shape["row"]),
        mesh=mesh,
        in_specs=(P("blk", "row"), P(("blk", "row"), None), P(("blk", "row"), None), P()),
        out_specs=(P(("blk", "row"), None), P(("blk", "row"))),
        check_vma=False,
    )
```

```python
import functools
import math

import jax
import jax.numpy as jnp
from jax import lax
from jax.experimental import pallas as pl
from jax.experimental.pallas import tpu as pltpu
from jax.sharding import PartitionSpec as P

MESH = pl.DeviceIdType.MESH
F32 = jnp.float32
BF16 = jnp.bfloat16
LANES = 256
SPAN = 4


def kernel(
    dims, n_row, x_ref, fine_ref, named_ref, heat_ref, out_ref, lse_ref,
    xbuf, panels, logits, norms, bias, top, peaks, total, weights, part, in_c, send_b, in_b,
    send_a, in_a, acc, mass_out, mass_in,
    x_send, x_recv, z_send, z_recv, gx_send, gx_recv, gc_send, gc_recv, c_send, c_recv,
    b_send, b_recv, a_send, a_recv, m_send, m_recv, own_sem,
):
    d0, d1, d2 = dims
    n_blk = d0 * d1 * d2
    row = lax.axis_index("row")
    blk = lax.axis_index("blk")
    i2 = lax.rem(blk, d2)
    i1 = lax.rem(lax.div(blk, d2), d1)
    i0 = lax.div(blk, d1 * d2)
    size = fine_ref.shape[0]
    width = fine_ref.shape[1]
    rows = xbuf.shape[1]
    feats = xbuf.shape[2]
    pair = d2 * size
    half = size // 2
    chunks = x_send.shape[1]
    step = rows // chunks
    blocks, names = named_ref.shape

    def near(i, o, d):
        return lax.rem(i + o + d, d)

    def index(a, b, c):
        return (a * d1 + b) * d2 + c

    def panel(owner):
        return panels.at[pl.ds(pl.multiple_of(owner * size, size), size), :]

    def remote(src, dst, send, recv, to, axis="blk"):
        return pltpu.make_async_remote_copy(
            src_ref=src, dst_ref=dst, send_sem=send, recv_sem=recv,
            device_id={axis: to}, device_id_type=MESH,
        )

    barrier = pltpu.get_barrier_semaphore()
    for d in range(1, n_row):
        pl.semaphore_signal(
            barrier, inc=1, device_id={"row": near(row, d, n_row)}, device_id_type=MESH
        )
    for d in range(1, n_blk):
        pl.semaphore_signal(
            barrier, inc=1, device_id={"blk": near(blk, d, n_blk)}, device_id_type=MESH
        )
    own_x = pltpu.make_async_copy(
        x_ref.at[pl.ds(pl.multiple_of(row * rows, rows), rows), :], xbuf.at[row], own_sem.at[0]
    )
    own_x.start()
    own_panel = pltpu.make_async_copy(fine_ref, panel(blk), own_sem.at[1])
    own_panel.start()
    pl.semaphore_wait(barrier, n_row - 1 + n_blk - 1)

    def z_copy(way, k, own=False):
        sign = 1 - 2 * way
        owner = index(i0 - sign * (k - 1), i1, i2)
        return remote(
            fine_ref if own else panel(owner), panel(owner),
            z_send.at[way, k - 1], z_recv.at[way, k - 1], index(i0 + sign, i1, i2),
        )

    def x_copy(a, o1, own=False):
        owner = index(a, i1, i2)
        return remote(
            fine_ref if own else panel(owner), panel(owner),
            gx_send.at[a, o1 - 1], gx_recv.at[a, o1 - 1], index(i0, near(i1, o1, d1), i2),
        )

    def c_copy(a, o1, o2, own=False):
        owner = index(a, near(i1, d1 - o1, d1), i2)
        return remote(
            fine_ref if own else panel(owner), panel(owner),
            gc_send.at[a, o1, o2 - 1], gc_recv.at[a, o1, o2 - 1],
            index(i0, i1, near(i2, o2, d2)),
        )

    def inside(i):
        return (i >= 0) & (i < d0)

    for o1 in range(1, d1):
        x_copy(i0, o1, True).start()
    for way in range(2):
        @pl.when(inside(i0 + 1 - 2 * way))
        def _():
            z_copy(way, 1, True).start()
    for o2 in range(1, d2):
        c_copy(i0, 0, o2, True).start()
    def x_points(d, c):
        to = near(row, d, n_row)
        return remote(
            x_ref.at[pl.ds(pl.multiple_of(to * rows + c * step, step), step), :],
            xbuf.at[row, pl.ds(pl.multiple_of(c * step, step), step), :],
            x_send.at[d - 1, c], x_recv.at[d - 1, c], to, "row",
        )

    for c in range(chunks):
        for d in range(1, n_row):
            x_points(d, c).start()

    @pl.loop(0, n_blk)
    def _(g):
        for b in range(blocks):
            hit = named_ref[b, 0] == g
            for j in range(1, names):
                hit = hit | (named_ref[b, j] == g)
            bias[g, :, b * (rows // blocks):(b + 1) * (rows // blocks)] = jnp.full(
                (1, rows // blocks), jnp.where(hit, 0.0, -1e30), F32
            )

    scale = 1.0 / (jnp.full((1, LANES), heat_ref[0], F32) * math.sqrt(width))
    top[...] = jnp.full(top.shape, -1e30, F32)
    total[...] = jnp.zeros(total.shape, F32)

    def measure(a, o1):
        for o2 in range(1, d2):
            c_copy(a, o1, o2).wait_recv()
        base = pl.multiple_of(index(a, near(i1, d1 - o1, d1), 0) * size, pair)
        whole = panels[pl.ds(base, pair), :].astype(F32)
        norms[pl.ds(base, pair), :] = jnp.broadcast_to(
            jnp.sum(whole * whole, axis=1, keepdims=True), (pair, 128)
        ) * scale[:, :128]
        return base

    def score(a, o1):
        base = measure(a, o1)
        left = panels[pl.ds(base, pair), pl.ds(pl.multiple_of(row * feats, feats), feats)]

        @pl.loop(0, rows // LANES)
        def _(c):
            lane = pl.multiple_of(c * LANES, LANES)
            logits[pl.ds(base, pair), pl.ds(lane, LANES)] = lax.dot_general(
                left, xbuf[row, pl.ds(lane, LANES), :], (((1,), (1,)), ((), ())),
                preferred_element_type=F32,
            )

    def z_event(way, k):
        sign = 1 - 2 * way

        @pl.when(inside(i0 - sign * k))
        def _():
            z_copy(way, k).wait_recv()
            @pl.when((k < d0 - 1) & inside(i0 + sign))
            def _():
                z_copy(way, k + 1).start()

            a = i0 - sign * k
            for o1 in range(1, d1):
                x_copy(a, o1).start()
            for o2 in range(1, d2):
                c_copy(a, 0, o2).start()

    def x_arrival(a):
        for o1 in range(1, d1):
            x_copy(a, o1).wait_recv()
            for o2 in range(1, d2):
                c_copy(a, o1, o2).start()

    def x_event(a):
        x_arrival(a)

        @pl.loop(0, d1)
        def _(o1):
            score(a, o1)

    joint = max(1, min(d1, SPAN // d2))

    def fuse(g, c, count, full=False):
        lanes = pl.ds(pl.multiple_of(c * LANES, LANES), LANES)
        base = pl.multiple_of(g * pair, pair)
        tile = pl.ds(base, count * pair)
        dots = None if full else logits[tile, lanes]
        for d in range(0 if full else 1, n_row):
            other = near(row, d, n_row)
            term = lax.dot_general(
                panels[tile, pl.ds(pl.multiple_of(other * feats, feats), feats)],
                xbuf[other, lanes, :], (((1,), (1,)), ((), ())),
                preferred_element_type=F32,
            )
            dots = term if dots is None else dots + term
        values = []
        old = top[0:1, lanes]
        best = jnp.broadcast_to(old, (8, LANES))
        for j in range(count * d2):
            norm = norms[pl.ds(base + j * size, size), :1]
            value = dots[j * size:(j + 1) * size] * (2.0 * scale) - norm
            values.append(value + bias[g * d2 + j, :, lanes])
            best = jnp.maximum(best, jnp.max(values[j].reshape(size // 8, 8, LANES), axis=0))
        best = jnp.max(best, axis=0, keepdims=True)
        added = total[:, lanes] * jnp.exp(old - best)
        for j in range(count * d2):
            value = jnp.exp(values[j] - best)
            logits[pl.ds(base + j * size, size), lanes] = value
            added = added + jnp.sum(value.reshape(size // 8, 8, LANES), axis=0)
        total[:, lanes] = added
        top[:, lanes] = jnp.broadcast_to(best, (8, LANES))
        for j in range(count):
            peaks[g + j, :, lanes] = best

    own_x.wait()
    own_panel.wait()
    late = jnp.where(i0 < d0 // 2, d0 - 1, 0)

    @pl.loop(1, d0)
    def _(k):
        for way in range(2):
            z_event(way, k)
        for way in range(2):
            a = i0 - (1 - 2 * way) * (k - 1)

            @pl.when(inside(a) & (a != late) & ((k > 1) | (way == 0)))
            def _():
                x_event(a)

    score(late, 0)

    each = d1 // joint
    first = jnp.where(late == 0, d1, 0)
    @pl.loop(0, chunks)
    def _(c):
        @pl.when(c == chunks - 1)
        def _():
            x_arrival(late)

        for d in range(1, n_row):
            x_points(d, c).wait_recv()
        fuse(late * d1 + i1, c, 1)

        @pl.loop(0, (d0 - 1) * each)
        def _(g):
            fuse(first + g * joint, c, joint)

    for o1 in range(1, d1):
        measure(late, o1)
        g = late * d1 + near(i1, -o1, d1)

        @pl.loop(0, chunks)
        def _(c):
            fuse(g, c, 1, True)

    summed = jnp.sum(total[...], axis=0, keepdims=True)
    lse_ref[...] = top[0:1, :] + jnp.log(summed)
    total[...] = jnp.broadcast_to(1.0 / summed, total.shape)

    def target(k):
        value = 0
        for z in range(d0):
            far = sorted(range(d0), key=lambda t: (-abs(t - z), t if z >= d0 // 2 else -t))
            value = jnp.where(i0 == z, far[k], value)
        return value

    targets = [target(k) for k in range(d0)]

    def c_sum(k, o1, o2):
        j = near(i2, o2, d2)
        return remote(
            part.at[k * d1 + o1, pl.ds(pl.multiple_of(j * size, size), size), :],
            in_c.at[k * d1 + o1, o2 - 1], c_send.at[k * d1 + o1, o2 - 1],
            c_recv.at[k * d1 + o1, o2 - 1], index(i0, i1, j),
        )

    def b_sum(k, o1, h):
        spot = pl.ds(h * half, half)
        return remote(
            send_b.at[k, o1 - 1, spot, :], in_b.at[k, o1 - 1, spot, :],
            b_send.at[k, o1 - 1, h], b_recv.at[k, o1 - 1, h],
            index(i0, near(i1, o1, d1), i2),
        )

    def a_sum(k, h, way, goal):
        spot = pl.ds(h * half, half)
        return remote(
            send_a.at[min(k, d0 - 2), spot, :], in_a.at[way, goal, spot, :],
            a_send.at[min(k, d0 - 2), h], a_recv.at[way, goal, h],
            index(near(i0, 1 - 2 * way, d0), i1, i2),
        )

    def m_sum(o0, o1, o2):
        to = index(near(i0, o0, d0), near(i1, o1, d1), near(i2, o2, d2))
        return remote(
            mass_out.at[to], mass_in.at[blk], m_send.at[o0, o1, o2], m_recv.at[o0, o1, o2], to
        )

    def weigh(k, o1):
        goal = targets[0]
        for other in range(1, d0):
            goal = jnp.where(k == other, targets[other], goal)
        owner = index(goal, near(i1, o1, d1), 0)
        base = pl.multiple_of(owner * size, pair)
        factor = jnp.exp(peaks[lax.div(owner, d2)] - top[0:1, :]) * total[0:1, :]
        weights[...] = (logits[pl.ds(base, pair), :] * factor).astype(BF16)

        @pl.loop(0, n_row)
        def _(s):
            part[k * d1 + o1, :, pl.ds(pl.multiple_of(s * feats, feats), feats)] = jnp.dot(
                weights[...], xbuf[s], preferred_element_type=F32
            ).astype(BF16)

        for o2 in range(1, d2):
            c_sum(k, o1, o2).start()
        mass = lax.dot_general(
            jnp.ones((8, rows), BF16), weights[...], (((1,), (1,)), ((), ())),
            preferred_element_type=F32,
        )
        for j in range(d2):
            mass_out[owner + j] = mass[:, j * size:(j + 1) * size]

    def chip_sum(k, o1, begin, count):
        start = pl.multiple_of(i2 * size + begin, half)
        value = part[k * d1 + o1, pl.ds(start, count), :].astype(F32)
        for o2 in range(1, d2):
            value = value + in_c[k * d1 + o1, o2 - 1, begin:begin + count, :].astype(F32)
        return value

    def ready(k, o1):
        for o2 in range(1, d2):
            c_sum(k, o1, o2).wait_recv()
        send_b[k, o1 - 1] = chip_sum(k, o1, 0, size).astype(BF16)
        for h in range(2):
            b_sum(k, o1, h).start()

    halves = [(k, h) for k in range(d0) for h in range(2)]

    jobs = d0 * (d1 - 1)

    def job(i):
        return lax.div(i, d1 - 1), 1 + lax.rem(i, d1 - 1)

    @pl.loop(0, jobs + 1)
    def _(i):
        k, o1 = job(i)
        end = i == jobs
        weigh(jnp.where(end, 0, k), jnp.where(end, 0, o1))

        @pl.when(i > 0)
        def _():
            ready(*job(i - 1))

    for position, (k, h) in enumerate(halves):
        for o1 in range(1, d1):
            b_sum(k, o1, h).wait_recv()
        if h == 0:
            for o2 in range(1, d2):
                c_sum(k, 0, o2).wait_recv()
        value = chip_sum(k, 0, h * half, half)
        for o1 in range(1, d1):
            value = value + in_b[k, o1 - 1, h * half:(h + 1) * half, :].astype(F32)
        spot = pl.ds(h * half, half)
        acc[spot, :] = value
        goal = targets[k]
        if k < d0 - 1:
            way = jnp.where(goal > i0, 0, 1)

            @pl.when(inside(i0 - 1 + 2 * way))
            def _():
                a_sum(k, h, way, goal).wait_recv()
                acc[spot, :] += in_a[way, goal, spot, :].astype(F32)

            send_a[k, spot, :] = acc[spot, :].astype(BF16)
            a_sum(k, h, way, goal).start()
            if h == 0:
                weigh(k + 1, 0)
                if k == d0 - 2:
                    for o0 in range(d0):
                        for o1 in range(d1):
                            for o2 in range(d2):
                                if (o0, o1, o2) != (0, 0, 0):
                                    m_sum(o0, o1, o2).start()

    mass_in[blk] = mass_out[blk]
    mass = None
    for o0 in range(d0):
        for o1 in range(d1):
            for o2 in range(d2):
                if (o0, o1, o2) != (0, 0, 0):
                    m_sum(o0, o1, o2).wait_recv()
    mass = mass_in[0]
    for g in range(1, n_blk):
        mass = mass + mass_in[g]
    column = jnp.broadcast_to(mass[0:1, :], (size, size)).T[:, 0:1] + 1.0
    acc[...] += panels[pl.ds(pl.multiple_of(blk * size, size), size), :].astype(F32)
    for h in range(2):
        spot = pl.ds(h * half, half)
        for way in range(2):
            @pl.when(inside(i0 - 1 + 2 * way))
            def _():
                a_sum(d0 - 1, h, way, i0).wait_recv()
                acc[spot, :] += in_a[way, i0, spot, :].astype(F32)
        out_ref[spot, :] = (acc[spot, :] / column[h * half:(h + 1) * half]).astype(BF16)

    for c in range(chunks):
        for d in range(1, n_row):
            x_points(d, c).wait_send()
    for way in range(2):
        sign = 1 - 2 * way
        for k in range(1, d0):
            @pl.when(inside(i0 + sign) & inside(i0 - sign * (k - 1)))
            def _():
                z_copy(way, k).wait_send()
    for a in range(d0):
        for o1 in range(1, d1):
            x_copy(a, o1).wait_send()
        for o1 in range(d1):
            for o2 in range(1, d2):
                c_copy(a, o1, o2).wait_send()
                c_sum(a, o1, o2).wait_send()
        for h in range(2):
            for o1 in range(1, d1):
                b_sum(a, o1, h).wait_send()
            if a < d0 - 1:
                a_sum(a, h, 0, i0).wait_send()
    for o0 in range(d0):
        for o1 in range(d1):
            for o2 in range(d2):
                if (o0, o1, o2) != (0, 0, 0):
                    m_sum(o0, o1, o2).wait_send()


def shards(n_blk, n_row, coarse, fine, candidates, heat):
    inner = 2 if n_blk < 32 else 4
    dims = (n_blk // (inner * inner), inner, inner)
    d0, d1, d2 = dims
    size, width = fine.shape
    rows = coarse.shape[0] // n_row
    feats = coarse.shape[1]
    vmem = pl.BlockSpec(memory_space=pltpu.VMEM)
    hbm = pl.BlockSpec(memory_space=pl.ANY)
    smem = pl.BlockSpec(memory_space=pltpu.SMEM)
    groups = d0 * d1
    chunks = rows // LANES
    dma = pltpu.SemaphoreType.DMA
    new, log_norm = pl.pallas_call(
        functools.partial(kernel, dims, n_row),
        out_shape=(
            jax.ShapeDtypeStruct((size, width), BF16),
            jax.ShapeDtypeStruct((1, rows), F32),
        ),
        in_specs=[hbm, hbm, smem, smem],
        out_specs=(vmem, vmem),
        scratch_shapes=[
            pltpu.VMEM((n_row, rows, feats), BF16),
            pltpu.VMEM((n_blk * size, width), BF16),
            pltpu.VMEM((n_blk * size, rows), F32),
            pltpu.VMEM((n_blk * size, 128), F32),
            pltpu.VMEM((n_blk, 1, rows), F32),
            pltpu.VMEM((8, rows), F32),
            pltpu.VMEM((groups, 1, rows), F32),
            pltpu.VMEM((8, rows), F32),
            pltpu.VMEM((d2 * size, rows), BF16),
            pltpu.VMEM((groups, d2 * size, width), BF16),
            pltpu.VMEM((groups, d2 - 1, size, width), BF16),
            pltpu.VMEM((d0, d1 - 1, size, width), BF16),
            pltpu.VMEM((d0, d1 - 1, size, width), BF16),
            pltpu.VMEM((d0 - 1, size, width), BF16),
            pltpu.VMEM((2, d0, size, width), BF16),
            pltpu.VMEM((size, width), F32),
            pltpu.VMEM((n_blk, 8, size), F32),
            pltpu.VMEM((n_blk, 8, size), F32),
            dma((n_row - 1, chunks)), dma((n_row - 1, chunks)),
            dma((2, d0 - 1)), dma((2, d0 - 1)),
            dma((d0, d1 - 1)), dma((d0, d1 - 1)),
            dma((d0, d1, d2 - 1)), dma((d0, d1, d2 - 1)),
            dma((groups, d2 - 1)), dma((groups, d2 - 1)),
            dma((d0, d1 - 1, 2)), dma((d0, d1 - 1, 2)),
            dma((d0 - 1, 2)), dma((2, d0, 2)),
            dma(dims), dma(dims),
            dma((2,)),
        ],
        compiler_params=pltpu.CompilerParams(
            collective_id=0, has_side_effects=True, vmem_limit_bytes=60 << 20
        ),
        cost_estimate=pl.CostEstimate(
            flops=4 * rows * n_blk * size * width, bytes_accessed=8 << 20,
            transcendentals=rows * n_blk * size,
        ),
    )(coarse, fine, candidates, heat)
    return new, log_norm.reshape(rows)


def solution(mesh):
    return jax.shard_map(
        functools.partial(shards, mesh.shape["blk"], mesh.shape["row"]),
        mesh=mesh,
        in_specs=(P("blk", "row"), P(("blk", "row"), None), P(("blk", "row"), None), P()),
        out_specs=(P(("blk", "row"), None), P(("blk", "row"))),
        check_vma=False,
    )
```
